32 devices in a mesh: grp: 2 (over x), gz: 8 (over z, y), col: 2 (over core).
Axes of the slice: x: 2, y: 2, z: 4, core: 2. Of those that a mesh axis runs over, the one named last changes fastest.
Arguments:
- noisy_image: float32 [4, 1024, 768], P('grp', 'gz', 'col'), parts along dimension 0, may hold values from -6 to 6
- fresh_noise: float32 [4, 1024, 768], P('grp', 'gz', 'col'), parts along dimension 0, may hold values from -6 to 6
- coil_maps: float32 [8, 4, 1024, 768], P('col', 'grp', 'gz'), parts along dimension 1, may hold values from -1.5 to 1.5
- measured: float32 [4, 768, 8, 1024], P('grp', 'gz', 'col'), parts along dimension 0, may hold values from -2.4 to 2.4
- sampled: int32 [768, 2048], P('gz', 'grp'), parts along dimension 1, may hold values 0 or 1
- first_kernel: bfloat16 [9, 64, 2], replicated, may hold values from -1.5 to 1.5
- inner_kernels: bfloat16 [1, 9, 64, 64], replicated, may hold values from -0.25 to 0.25
- last_kernel: bfloat16 [9, 2, 64], replicated, may hold values from -0.25 to 0.25
Outputs:
- next_image: float32 [4, 1024, 768], P('grp', 'gz', 'col'), parts along dimension 0
The draws below stay inside these ranges and needn't reach their ends.
There are 2 independent parts, one for each index of `grp`. The reference program is written for one: setup_inputs(seed, part) draws one part's arguments, and reference() takes and returns one part's arrays. A program takes and returns all parts, laid end to end along the dimension named above; an argument that names none is the same for every part. Nothing has to cross between parts.
All inputs are finite; a program needn't handle non-finite values. No bound on the sum of `sampled` on one device may be relied on, other than what follows from the above.
Results may differ from the reference program's by a relative error of at most 0.00044.
Values may be sent and summed in bfloat16 or wider, within the bound.
A program may use at most 128 MiB of HBM per device.

```python
import jax
import jax.numpy as jnp
from jax import lax

H = 1024
W = 768
CH = 64
COILS = 8
MID_LAYERS = 1


def place_ends(values, stream_key, low, top_value):
    longest = values.shape.index(max(values.shape))
    spots = []
    for shift in (0, 1):
        where = [jax.random.randint(jax.random.fold_in(stream_key, axis), (), 0, length) for axis, length in enumerate(values.shape)]
        where[longest] = (where[longest] + shift) % values.shape[longest]
        spots.append(tuple(where))
    return values.at[spots[0]].set(low).at[spots[1]].set(top_value)


def block_levels(key, dims, shards, smallest, largest):
    factor_of = 1.0
    for dim, shards_of in shards:
        draws = jax.random.uniform(jax.random.fold_in(jax.random.fold_in(key, 6), dim), (shards_of,), jnp.float32, smallest / len(shards), largest / len(shards))
        factor_of = factor_of * jnp.repeat(jnp.exp(draws), dims[dim] // shards_of).reshape((-1,) + (1,) * (len(dims) - 1 - dim))
    return factor_of


def normal_values(own_key, dims, width, reach, shards=(), dtype=jnp.bfloat16):
    gain = block_levels(own_key, dims, shards, -0.22, 0.18) if shards else 1.0
    entries = jax.random.normal(own_key, dims, jnp.float32) * width * gain
    return jnp.minimum(jnp.maximum(entries, -reach), reach).astype(dtype)


def setup_inputs(seed: int = 0, part: int = 0) -> dict:
    splits = jax.random.split(jax.random.key(seed), 9)
    own_keys = jax.random.split(jax.random.fold_in(splits[8], part), 9)
    return {
        "noisy_image": normal_values(own_keys[0], (2, H, W), 1.0, 6.0, ((1, 8), (2, 2)), jnp.float32),
        "fresh_noise": normal_values(own_keys[1], (2, H, W), 1.0, 6.0, ((1, 8), (2, 2)), jnp.float32),
        "coil_maps": normal_values(own_keys[2], (COILS, 2, H, W), 0.25, 1.5, ((0, 2), (2, 8)), jnp.float32),
        "measured": normal_values(own_keys[3], (2, W, COILS, H), 0.4, 2.4, ((1, 8), (2, 2)), jnp.float32),
        "sampled": place_ends((jax.random.randint(own_keys[4], (W, H), 0, 3) < 1).astype(jnp.int32), jax.random.fold_in(own_keys[4], 1), 0, 1),
        "first_kernel": normal_values(splits[5], (9, CH, 2), (9 * 2) ** -0.5, 1.5),
        "inner_kernels": normal_values(splits[6], (MID_LAYERS, 9, CH, CH), (9 * CH) ** -0.5, 0.25),
        "last_kernel": normal_values(splits[7], (9, 2, CH), (9 * CH) ** -0.5, 0.25),
    }


SCALE_NOW = 0.8
SIGMA_NOW = 0.6
STEP_GAIN = 1.0
SCALE_NEXT = 0.9
DIRECT_GAIN = 0.31622776601683794
NOISE_GAIN = 0.3


def convolve(features, kernel):
    kernel_out = kernel.shape[1]
    kernel_in = kernel.shape[2]
    filters = jnp.transpose(kernel.astype(jnp.float32).reshape(3, 3, kernel_out, kernel_in), (2, 3, 0, 1))
    result = lax.conv_general_dilated(features.astype(jnp.float32)[None], filters, (1, 1), ((1, 1), (1, 1)), dimension_numbers=("NCHW", "OIHW", "NCHW"), precision=lax.Precision.HIGHEST)
    return result[0]


def reference(noisy_image, fresh_noise, coil_maps, measured, sampled, first_kernel, inner_kernels, last_kernel):
    hidden = jax.nn.silu(convolve(noisy_image.astype(jnp.bfloat16), first_kernel)).astype(jnp.bfloat16)
    for layer_index in range(MID_LAYERS):
        hidden = jax.nn.silu(convolve(hidden, inner_kernels[layer_index])).astype(jnp.bfloat16)
    predicted = convolve(hidden, last_kernel)
    clean = (noisy_image - SIGMA_NOW * predicted) / SCALE_NOW
    maps_real = coil_maps[:, 0]
    maps_imag = coil_maps[:, 1]
    coil_real = maps_real * clean[0] - maps_imag * clean[1]
    coil_imag = maps_real * clean[1] + maps_imag * clean[0]
    spectra = jnp.fft.fft2(lax.complex(coil_real, coil_imag), norm="ortho")
    target = lax.complex(jnp.transpose(measured[0], (1, 2, 0)), jnp.transpose(measured[1], (1, 2, 0)))
    keeping = jnp.transpose(sampled).astype(jnp.float32)
    residual = (spectra - target) * keeping
    back = jnp.fft.ifft2(residual, norm="ortho")
    back_real = jnp.real(back)
    back_imag = jnp.imag(back)
    grad_real = jnp.sum(maps_real * back_real + maps_imag * back_imag, axis=0)
    grad_imag = jnp.sum(maps_real * back_imag - maps_imag * back_real, axis=0)
    update = clean - STEP_GAIN * jnp.stack([grad_real, grad_imag])
    return SCALE_NEXT * update + DIRECT_GAIN * predicted + NOISE_GAIN * fresh_noise
```

```python
from functools import partial
import math

import jax
import jax.numpy as jnp
from jax import lax
from jax.experimental import pallas as pl
from jax.experimental.pallas import tpu as pltpu
from jax.sharding import PartitionSpec as P

H_FAC = 8
W_FAC = 6
ROWS = 4


SCALE_NOW = 0.8
SIGMA_NOW = 0.6
STEP_GAIN = 1.0
SCALE_NEXT = 0.9
DIRECT_GAIN = 0.31622776601683794
NOISE_GAIN = 0.3


def with_halo(block, sides, width):
    for axis, dim in sides:
        count = lax.axis_size(axis)
        forward = [(i, i + 1) for i in range(count - 1)]
        backward = [(target, source) for source, target in forward]
        low = lax.ppermute(
            lax.slice_in_dim(block, block.shape[dim] - width, None, axis=dim), axis, forward
        )
        high = lax.ppermute(lax.slice_in_dim(block, 0, width, axis=dim), axis, backward)
        block = jnp.concatenate([low, block, high], axis=dim)
    return block


def row_banded(kernel, span):
    taps = kernel.reshape(3, 3, kernel.shape[1], kernel.shape[2])
    return jnp.stack(
        [
            jnp.pad(taps, ((start, span - 3 - start), (0, 0), (0, 0), (0, 0)))
            for start in range(span - 2)
        ]
    )


def network_kernel(
    groups,
    cols,
    tiles_ref,
    first_ref,
    inner_ref,
    last_ref,
    first_rows_ref,
    inner_rows_ref,
    inside_ref,
    out_ref,
    first_held,
    inner_held,
):
    frame, width = inside_ref.shape
    half = width // 2

    def act(halved, keep):
        return (halved + halved * jnp.tanh(halved)) * (inside_ref[...] * keep)

    def first_layer(group):
        halved = jnp.dot(
            tiles_ref[group // ROWS],
            first_ref[lax.rem(group, ROWS)],
            preferred_element_type=jnp.float32,
        )
        hidden = act(halved, first_rows_ref[group])
        slot = lax.rem(group, ROWS)
        first_held[slot, 0] = pltpu.roll(hidden, 1, 0).astype(jnp.bfloat16)
        first_held[slot, 1] = hidden.astype(jnp.bfloat16)
        first_held[slot, 2] = pltpu.roll(hidden, frame - 1, 0).astype(jnp.bfloat16)

    def inner_layer(group):
        slot = lax.rem(group, ROWS)
        after = lax.rem(group + 1, ROWS)
        total = None
        for shift in range(3):
            part = jnp.dot(
                first_held[slot, shift],
                inner_ref[shift, :width],
                preferred_element_type=jnp.float32,
            ) + jnp.dot(
                first_held[after, shift, :, :half],
                inner_ref[shift, width:],
                preferred_element_type=jnp.float32,
            )
            total = part if total is None else total + part
        inner_held[slot] = act(total, inner_rows_ref[group]).astype(jnp.bfloat16)

    def last_layer(group):
        slot = lax.rem(group, ROWS)
        after = lax.rem(group + 1, ROWS)
        lanes = (((1,), (1,)), ((), ()))
        part = lax.dot_general(
            last_ref[:, :width], inner_held[slot], lanes, preferred_element_type=jnp.float32
        ) + lax.dot_general(
            last_ref[:, width:],
            inner_held[after, :, :half],
            lanes,
            preferred_element_type=jnp.float32,
        )
        left = part[:8]
        left = jnp.concatenate([left[:, frame - 1 :], left[:, : cols - 1]], axis=1)
        out_ref[group] = left + part[8:16, :cols] + part[16:24, 1 : cols + 1]

    for group in range(4):
        first_layer(group)
    for group in range(2):
        inner_layer(group)

    def step(group, carry):
        last_layer(group)
        inner_layer(group + 2)
        first_layer(group + 4)
        return carry

    lax.fori_loop(0, groups, step, 0)


def network(image, first_kernel, inner_kernels, last_kernel):
    channels, rows, cols = image.shape
    hidden = first_kernel.shape[1]
    groups = rows // ROWS
    frame = cols + 16
    width = ROWS * hidden
    span = ROWS * ROWS + 2
    tile_count = groups // ROWS + 1
    padded = with_halo(image.astype(jnp.bfloat16), (("gz", 1), ("col", 2)), 3)
    padded = jnp.pad(padded, ((0, 0), (0, ROWS * ROWS * tile_count + 2 - rows - 6), (0, 0)))
    gap = jnp.zeros(padded.shape[:2] + (frame - cols - 6,), padded.dtype)
    ring = jnp.concatenate([padded[:, :, 3:], gap, padded[:, :, :3]], axis=2)
    shifted = jnp.stack([jnp.roll(ring, 1 - shift, axis=2) for shift in range(3)])
    tiles = jnp.stack(
        [shifted[:, :, ROWS * ROWS * t : ROWS * ROWS * t + span] for t in range(tile_count)]
    )
    depth = 3 * channels * span
    tiles = jnp.transpose(tiles.reshape(tile_count, depth, frame), (0, 2, 1))
    tiles = jnp.pad(tiles, ((0, 0), (0, 0), (0, 128 - depth)))
    half = jnp.asarray(0.5, jnp.bfloat16)
    first = jnp.transpose(row_banded(first_kernel * half, span), (2, 4, 1, 0, 3))
    first = first.reshape(depth, ROWS, width)
    first = jnp.pad(jnp.transpose(first, (1, 0, 2)), ((0, 0), (0, 128 - depth), (0, 0)))
    inner = jnp.transpose(row_banded(inner_kernels[0] * half, ROWS + 2), (2, 1, 4, 0, 3))
    inner = inner.reshape(3, (ROWS + 2) * hidden, width)
    last = jnp.transpose(row_banded(last_kernel, ROWS + 2), (2, 0, 3, 1, 4))
    last = last.reshape(3 * ROWS * channels, (ROWS + 2) * hidden)
    last = jnp.pad(last, ((0, 32 - last.shape[0]), (0, 0)))
    top = lax.axis_index("gz") * rows
    height = rows * lax.axis_size("gz")
    across = cols * lax.axis_size("col")

    def row_mask(count, offset):
        place = top + ROWS * jnp.arange(count)[:, None] + jnp.arange(ROWS)[None, :] - offset
        keep = ((place >= 0) & (place < height)).astype(jnp.float32)
        return jnp.repeat(keep, hidden, axis=1).reshape(count, 1, width)

    spot = jnp.arange(frame)
    spot = jnp.where(spot < cols + 8, spot, spot - frame) + lax.axis_index("col") * cols
    inside = ((spot >= 0) & (spot < across)).astype(jnp.float32)
    inside = jnp.broadcast_to(inside[:, None], (frame, width))
    result = pl.pallas_call(
        partial(network_kernel, groups, cols),
        out_shape=jax.ShapeDtypeStruct((groups, ROWS * channels, cols), jnp.float32),
        in_specs=[pl.BlockSpec(memory_space=pltpu.VMEM)] * 7,
        out_specs=pl.BlockSpec(memory_space=pltpu.VMEM),
        scratch_shapes=[
            pltpu.VMEM((ROWS, 3, frame, width), jnp.bfloat16),
            pltpu.VMEM((ROWS, frame, width), jnp.bfloat16),
        ],
        compiler_params=pltpu.CompilerParams(vmem_limit_bytes=40 * 1024 * 1024),
        name="network",
    )(tiles, first, inner, last, row_mask(groups + 4, 2), row_mask(groups + 2, 1), inside)
    result = result.reshape(groups, ROWS, channels, cols)
    return jnp.transpose(result, (2, 0, 1, 3)).reshape(channels, rows, cols)


def rotation(rows_len, cols_len, modulus, direction):
    first_index = jnp.arange(rows_len, dtype=jnp.int32)
    second_index = jnp.arange(cols_len, dtype=jnp.int32)
    phase_index = first_index[:, None] * second_index[None, :] % modulus
    angles = phase_index.astype(jnp.float32) * (direction * 2.0 * math.pi / modulus)
    return (jnp.cos(angles), jnp.sin(angles))


def complex_dot(matrix_pair, data_pair, contracting):
    product = partial(
        lax.dot_general,
        dimension_numbers=(contracting, ((), ())),
        precision=lax.Precision.HIGH,
        preferred_element_type=jnp.float32,
    )
    return (
        product(matrix_pair[0], data_pair[0]) - product(matrix_pair[1], data_pair[1]),
        product(matrix_pair[0], data_pair[1]) + product(matrix_pair[1], data_pair[0]),
    )


def complex_mul(first_pair, second_pair):
    return (
        first_pair[0] * second_pair[0] - first_pair[1] * second_pair[1],
        first_pair[0] * second_pair[1] + first_pair[1] * second_pair[0],
    )


def transform_last(data_pair, outer_len, direction):
    vectors, length = data_pair[0].shape
    inner_len = length // outer_len
    shaped = (
        data_pair[0].reshape(vectors, outer_len, inner_len),
        data_pair[1].reshape(vectors, outer_len, inner_len),
    )
    sectioned = complex_dot(
        rotation(outer_len, outer_len, outer_len, direction), shaped, ((1,), (1,))
    )
    twiddles = rotation(outer_len, inner_len, length, direction)
    twisted = complex_mul(sectioned, (twiddles[0][:, None, :], twiddles[1][:, None, :]))
    finished = complex_dot(
        rotation(inner_len, inner_len, inner_len, direction), twisted, ((1,), (2,))
    )
    factor = 1.0 / math.sqrt(length)
    return (
        finished[0].reshape(length, vectors) * factor,
        finished[1].reshape(length, vectors) * factor,
    )


def transform_first(data_pair, outer_len, direction):
    length, vectors = data_pair[0].shape
    inner_len = length // outer_len
    shaped = (
        data_pair[0].reshape(outer_len, inner_len, vectors),
        data_pair[1].reshape(outer_len, inner_len, vectors),
    )
    sectioned = complex_dot(
        rotation(outer_len, outer_len, outer_len, direction), shaped, ((1,), (0,))
    )
    twiddles = rotation(outer_len, inner_len, length, direction)
    twisted = complex_mul(sectioned, (twiddles[0][:, :, None], twiddles[1][:, :, None]))
    finished = complex_dot(
        rotation(inner_len, inner_len, inner_len, direction), twisted, ((1,), (1,))
    )
    factor = 1.0 / math.sqrt(length)
    return (
        finished[0].reshape(length, vectors) * factor,
        finished[1].reshape(length, vectors) * factor,
    )


def local(
    noisy_image, fresh_noise, coil_maps, measured, sampled, first_kernel, inner_kernels, last_kernel
):
    predicted = network(noisy_image, first_kernel, inner_kernels, last_kernel)
    clean = (noisy_image - SIGMA_NOW * predicted) / SCALE_NOW
    clean_wide = lax.all_gather(clean, "col", axis=2, tiled=True)
    maps_real = coil_maps[:, 0]
    maps_imag = coil_maps[:, 1]
    coil_count, row_count, full_cols = maps_real.shape
    coil_pair = complex_mul((maps_real, maps_imag), (clean_wide[0][None], clean_wide[1][None]))
    spectra = transform_last(
        (
            coil_pair[0].reshape(coil_count * row_count, full_cols),
            coil_pair[1].reshape(coil_count * row_count, full_cols),
        ),
        W_FAC,
        -1.0,
    )
    groups = lax.axis_size("gz")
    pencil = full_cols // groups
    arrived = (
        lax.all_to_all(
            spectra[0].reshape(groups, pencil, coil_count, row_count),
            "gz",
            split_axis=0,
            concat_axis=3,
            tiled=True,
        ),
        lax.all_to_all(
            spectra[1].reshape(groups, pencil, coil_count, row_count),
            "gz",
            split_axis=0,
            concat_axis=3,
            tiled=True,
        ),
    )
    item_count = arrived[0].shape[2]
    height = arrived[0].shape[3]
    flattened = (
        arrived[0].reshape(pencil * item_count, height),
        arrived[1].reshape(pencil * item_count, height),
    )
    transformed = transform_last(flattened, H_FAC, -1.0)
    keeping = sampled.astype(jnp.float32)[:, None, :]
    resid_real = keeping * (transformed[0].T.reshape(pencil, item_count, height) - measured[0])
    resid_imag = keeping * (transformed[1].T.reshape(pencil, item_count, height) - measured[1])
    height = resid_real.shape[2]
    inverse = transform_last(
        (
            resid_real.reshape(pencil * coil_count, height),
            resid_imag.reshape(pencil * coil_count, height),
        ),
        H_FAC,
        1.0,
    )
    arrived = (
        lax.all_to_all(
            inverse[0].T.reshape(pencil, coil_count, groups, row_count),
            "gz",
            split_axis=2,
            concat_axis=0,
            tiled=True,
        ),
        lax.all_to_all(
            inverse[1].T.reshape(pencil, coil_count, groups, row_count),
            "gz",
            split_axis=2,
            concat_axis=0,
            tiled=True,
        ),
    )
    item_count = arrived[0].shape[1]
    flattened = (
        arrived[0].reshape(full_cols, item_count * row_count),
        arrived[1].reshape(full_cols, item_count * row_count),
    )
    transformed = transform_first(flattened, W_FAC, 1.0)
    back_real = jnp.transpose(transformed[0].reshape(full_cols, item_count, row_count), (1, 2, 0))
    back_imag = jnp.transpose(transformed[1].reshape(full_cols, item_count, row_count), (1, 2, 0))
    grad_real = jnp.sum(maps_real * back_real + maps_imag * back_imag, axis=0)
    grad_imag = jnp.sum(maps_real * back_imag - maps_imag * back_real, axis=0)
    grad_tile = lax.psum_scatter(
        jnp.stack([grad_real, grad_imag]), "col", scatter_dimension=2, tiled=True
    )
    update = clean - STEP_GAIN * grad_tile
    return SCALE_NEXT * update + DIRECT_GAIN * predicted + NOISE_GAIN * fresh_noise


def solution(mesh):
    in_specs = (
        P("grp", "gz", "col"),
        P("grp", "gz", "col"),
        P("col", "grp", "gz", None),
        P("grp", "gz", "col", None),
        P("gz", "grp"),
        P(),
        P(),
        P(),
    )
    out_specs = P("grp", "gz", "col")
    return jax.shard_map(local, mesh=mesh, in_specs=in_specs, out_specs=out_specs, check_vma=False)
```

```python
from functools import partial
import math

import jax
import jax.numpy as jnp
import numpy as np
from jax import lax
from jax.experimental import pallas as pl
from jax.experimental.pallas import tpu as pltpu
from jax.sharding import PartitionSpec as P

H_FAC = 8
W_FAC = 6
ROWS = 4


SCALE_NOW = 0.8
SIGMA_NOW = 0.6
STEP_GAIN = 1.0
SCALE_NEXT = 0.9
DIRECT_GAIN = 0.31622776601683794
NOISE_GAIN = 0.3


def with_halo(block, sides, width):
    for axis, dim in sides:
        count = lax.axis_size(axis)
        forward = [(i, i + 1) for i in range(count - 1)]
        backward = [(target, source) for source, target in forward]
        low = lax.ppermute(
            lax.slice_in_dim(block, block.shape[dim] - width, None, axis=dim), axis, forward
        )
        high = lax.ppermute(lax.slice_in_dim(block, 0, width, axis=dim), axis, backward)
        block = jnp.concatenate([low, block, high], axis=dim)
    return block


def row_banded(kernel, span):
    taps = kernel.reshape(3, 3, kernel.shape[1], kernel.shape[2])
    return jnp.stack(
        [
            jnp.pad(taps, ((start, span - 3 - start), (0, 0), (0, 0), (0, 0)))
            for start in range(span - 2)
        ]
    )


def network_kernel(
    groups,
    cols,
    tiles_ref,
    first_ref,
    inner_ref,
    last_ref,
    first_rows_ref,
    inner_rows_ref,
    inside_ref,
    out_ref,
    first_held,
    inner_held,
):
    frame, width = inside_ref.shape
    half = width // 2

    def act(halved, keep):
        return (halved + halved * jnp.tanh(halved)) * (inside_ref[...] * keep)

    def first_layer(group):
        halved = jnp.dot(
            tiles_ref[group // ROWS],
            first_ref[lax.rem(group, ROWS)],
            preferred_element_type=jnp.float32,
        )
        hidden = act(halved, first_rows_ref[group])
        slot = lax.rem(group, ROWS)
        first_held[slot, 0] = pltpu.roll(hidden, 1, 0).astype(jnp.bfloat16)
        first_held[slot, 1] = hidden.astype(jnp.bfloat16)
        first_held[slot, 2] = pltpu.roll(hidden, frame - 1, 0).astype(jnp.bfloat16)

    def inner_layer(group):
        slot = lax.rem(group, ROWS)
        after = lax.rem(group + 1, ROWS)
        total = None
        for shift in range(3):
            part = jnp.dot(
                first_held[slot, shift],
                inner_ref[shift, :width],
                preferred_element_type=jnp.float32,
            ) + jnp.dot(
                first_held[after, shift, :, :half],
                inner_ref[shift, width:],
                preferred_element_type=jnp.float32,
            )
            total = part if total is None else total + part
        inner_held[slot] = act(total, inner_rows_ref[group]).astype(jnp.bfloat16)

    def last_layer(group):
        slot = lax.rem(group, ROWS)
        after = lax.rem(group + 1, ROWS)
        lanes = (((1,), (1,)), ((), ()))
        part = lax.dot_general(
            last_ref[:, :width], inner_held[slot], lanes, preferred_element_type=jnp.float32
        ) + lax.dot_general(
            last_ref[:, width:],
            inner_held[after, :, :half],
            lanes,
            preferred_element_type=jnp.float32,
        )
        left = part[:8]
        left = jnp.concatenate([left[:, frame - 1 :], left[:, : cols - 1]], axis=1)
        out_ref[group] = left + part[8:16, :cols] + part[16:24, 1 : cols + 1]

    for group in range(4):
        first_layer(group)
    for group in range(2):
        inner_layer(group)

    def step(group, carry):
        last_layer(group)
        inner_layer(group + 2)
        first_layer(group + 4)
        return carry

    lax.fori_loop(0, groups, step, 0)


def network(image, first_kernel, inner_kernels, last_kernel):
    channels, rows, cols = image.shape
    hidden = first_kernel.shape[1]
    groups = rows // ROWS
    frame = cols + 16
    width = ROWS * hidden
    span = ROWS * ROWS + 2
    tile_count = groups // ROWS + 1
    padded = with_halo(image.astype(jnp.bfloat16), (("gz", 1), ("col", 2)), 3)
    padded = jnp.pad(padded, ((0, 0), (0, ROWS * ROWS * tile_count + 2 - rows - 6), (0, 0)))
    gap = jnp.zeros(padded.shape[:2] + (frame - cols - 6,), padded.dtype)
    ring = jnp.concatenate([padded[:, :, 3:], gap, padded[:, :, :3]], axis=2)
    shifted = jnp.stack([jnp.roll(ring, 1 - shift, axis=2) for shift in range(3)])
    tiles = jnp.stack(
        [shifted[:, :, ROWS * ROWS * t : ROWS * ROWS * t + span] for t in range(tile_count)]
    )
    depth = 3 * channels * span
    tiles = jnp.transpose(tiles.reshape(tile_count, depth, frame), (0, 2, 1))
    tiles = jnp.pad(tiles, ((0, 0), (0, 0), (0, 128 - depth)))
    half = jnp.asarray(0.5, jnp.bfloat16)
    first = jnp.transpose(row_banded(first_kernel * half, span), (2, 4, 1, 0, 3))
    first = first.reshape(depth, ROWS, width)
    first = jnp.pad(jnp.transpose(first, (1, 0, 2)), ((0, 0), (0, 128 - depth), (0, 0)))
    inner = jnp.transpose(row_banded(inner_kernels[0] * half, ROWS + 2), (2, 1, 4, 0, 3))
    inner = inner.reshape(3, (ROWS + 2) * hidden, width)
    last = jnp.transpose(row_banded(last_kernel, ROWS + 2), (2, 0, 3, 1, 4))
    last = last.reshape(3 * ROWS * channels, (ROWS + 2) * hidden)
    last = jnp.pad(last, ((0, 32 - last.shape[0]), (0, 0)))
    top = lax.axis_index("gz") * rows
    height = rows * lax.axis_size("gz")
    across = cols * lax.axis_size("col")

    def row_mask(count, offset):
        place = top + ROWS * jnp.arange(count)[:, None] + jnp.arange(ROWS)[None, :] - offset
        keep = ((place >= 0) & (place < height)).astype(jnp.float32)
        return jnp.repeat(keep, hidden, axis=1).reshape(count, 1, width)

    spot = jnp.arange(frame)
    spot = jnp.where(spot < cols + 8, spot, spot - frame) + lax.axis_index("col") * cols
    inside = ((spot >= 0) & (spot < across)).astype(jnp.float32)
    inside = jnp.broadcast_to(inside[:, None], (frame, width))
    result = pl.pallas_call(
        partial(network_kernel, groups, cols),
        out_shape=jax.ShapeDtypeStruct((groups, ROWS * channels, cols), jnp.float32),
        in_specs=[pl.BlockSpec(memory_space=pltpu.VMEM)] * 7,
        out_specs=pl.BlockSpec(memory_space=pltpu.VMEM),
        scratch_shapes=[
            pltpu.VMEM((ROWS, 3, frame, width), jnp.bfloat16),
            pltpu.VMEM((ROWS, frame, width), jnp.bfloat16),
        ],
        compiler_params=pltpu.CompilerParams(vmem_limit_bytes=40 * 1024 * 1024),
        name="network",
    )(tiles, first, inner, last, row_mask(groups + 4, 2), row_mask(groups + 2, 1), inside)
    result = result.reshape(groups, ROWS, channels, cols)
    return jnp.transpose(result, (2, 0, 1, 3)).reshape(channels, rows, cols)


def rotation(rows_len, cols_len, modulus, direction):
    first_index = jnp.arange(rows_len, dtype=jnp.int32)
    second_index = jnp.arange(cols_len, dtype=jnp.int32)
    phase_index = first_index[:, None] * second_index[None, :] % modulus
    angles = phase_index.astype(jnp.float32) * (direction * 2.0 * math.pi / modulus)
    return (jnp.cos(angles), jnp.sin(angles))


def complex_dot(matrix_pair, data_pair, contracting):
    product = partial(
        lax.dot_general,
        dimension_numbers=(contracting, ((), ())),
        precision=lax.Precision.HIGH,
        preferred_element_type=jnp.float32,
    )
    return (
        product(matrix_pair[0], data_pair[0]) - product(matrix_pair[1], data_pair[1]),
        product(matrix_pair[0], data_pair[1]) + product(matrix_pair[1], data_pair[0]),
    )


def complex_mul(first_pair, second_pair):
    return (
        first_pair[0] * second_pair[0] - first_pair[1] * second_pair[1],
        first_pair[0] * second_pair[1] + first_pair[1] * second_pair[0],
    )


def transform_last(data_pair, outer_len, direction):
    vectors, length = data_pair[0].shape
    inner_len = length // outer_len
    shaped = (
        data_pair[0].reshape(vectors, outer_len, inner_len),
        data_pair[1].reshape(vectors, outer_len, inner_len),
    )
    sectioned = complex_dot(
        rotation(outer_len, outer_len, outer_len, direction), shaped, ((1,), (1,))
    )
    twiddles = rotation(outer_len, inner_len, length, direction)
    twisted = complex_mul(sectioned, (twiddles[0][:, None, :], twiddles[1][:, None, :]))
    finished = complex_dot(
        rotation(inner_len, inner_len, inner_len, direction), twisted, ((1,), (2,))
    )
    factor = 1.0 / math.sqrt(length)
    return (
        finished[0].reshape(length, vectors) * factor,
        finished[1].reshape(length, vectors) * factor,
    )


def transform_first(data_pair, outer_len, direction):
    length, vectors = data_pair[0].shape
    inner_len = length // outer_len
    shaped = (
        data_pair[0].reshape(outer_len, inner_len, vectors),
        data_pair[1].reshape(outer_len, inner_len, vectors),
    )
    sectioned = complex_dot(
        rotation(outer_len, outer_len, outer_len, direction), shaped, ((1,), (0,))
    )
    twiddles = rotation(outer_len, inner_len, length, direction)
    twisted = complex_mul(sectioned, (twiddles[0][:, :, None], twiddles[1][:, :, None]))
    finished = complex_dot(
        rotation(inner_len, inner_len, inner_len, direction), twisted, ((1,), (1,))
    )
    factor = 1.0 / math.sqrt(length)
    return (
        finished[0].reshape(length, vectors) * factor,
        finished[1].reshape(length, vectors) * factor,
    )


def split_pair(real, imag, axis):
    both = jnp.concatenate([real, imag], axis=axis)
    high = both.astype(jnp.bfloat16)
    low = (both - high.astype(jnp.float32)).astype(jnp.bfloat16)
    return jnp.concatenate([high, low, high], axis=axis)


def pair_matrix(inner, length, transposed):
    angles = np.outer(np.arange(inner), np.arange(inner)) % inner * (2.0 * np.pi / inner)
    cosines, sines = np.cos(angles), np.sin(angles)
    matrix = np.block([[cosines, sines], [-sines, cosines]]) / np.sqrt(length)
    if transposed:
        matrix = matrix.T
    high = matrix.astype(jnp.bfloat16)
    low = (matrix - high.astype(np.float64)).astype(jnp.bfloat16)
    return high, low


def twiddle_rows(outer, inner):
    angles = np.outer(np.arange(outer), np.arange(inner)) * (2.0 * np.pi / (outer * inner))
    return np.stack([np.cos(angles), np.sin(angles)], axis=1).astype(np.float32)


def turn(pair, twiddle_ref, index, sign):
    if index == 0:
        return pair
    cosine = twiddle_ref[index, 0:1]
    sine = sign * twiddle_ref[index, 1:2]
    return (pair[0] * cosine - pair[1] * sine, pair[0] * sine + pair[1] * cosine)


def level_out(out_ref, body_rows):
    values = out_ref[:, :body_rows, :]
    top = jnp.max(jnp.max(jnp.abs(values), axis=0), axis=0, keepdims=True)
    top = jnp.maximum(jnp.max(top, axis=1, keepdims=True), 1e-30)
    power = jnp.ceil(jnp.log2(top)) - 13.0
    out_ref[:, :body_rows, :] = values * jnp.exp2(-power)
    tail = out_ref.shape[1] - body_rows
    out_ref[:, body_rows:, :] = jnp.broadcast_to(
        power[None], (out_ref.shape[0], tail, out_ref.shape[2])
    )


def columns_kernel(clean_ref, maps_ref, matrix_ref, twiddle_ref, out_ref):
    coils, _, rows, full = maps_ref.shape
    groups = out_ref.shape[0]
    inner = full // 3
    piece = inner // groups
    root = math.sqrt(0.75)
    clean = (clean_ref[0], clean_ref[1])
    for start in range(0, coils, 2):
        image = [
            complex_mul((maps_ref[coil, 0], maps_ref[coil, 1]), clean)
            for coil in (start, start + 1)
        ]
        image = [jnp.concatenate([image[0][part], image[1][part]], axis=0) for part in range(2)]
        first, second, third = [
            (image[0][:, n * inner : (n + 1) * inner], image[1][:, n * inner : (n + 1) * inner])
            for n in range(3)
        ]
        total = (second[0] + third[0], second[1] + third[1])
        apart = (root * (second[0] - third[0]), root * (second[1] - third[1]))
        middle = (first[0] - 0.5 * total[0], first[1] - 0.5 * total[1])
        bins = (
            (first[0] + total[0], first[1] + total[1]),
            (middle[0] + apart[1], middle[1] - apart[0]),
            (middle[0] - apart[1], middle[1] + apart[0]),
        )
        for index in range(3):
            turned = turn(bins[index], twiddle_ref, index, -1.0)
            result = lax.dot_general(
                matrix_ref[...],
                split_pair(turned[0], turned[1], 1),
                (((1,), (1,)), ((), ())),
                preferred_element_type=jnp.float32,
            )
            for part in range(2):
                for which in range(2):
                    base = ((part * coils + start + which) * 3 + index) * piece
                    block = result[part * inner : (part + 1) * inner]
                    block = block[:, which * rows : (which + 1) * rows]
                    out_ref[:, base : base + piece, :] = block.reshape(groups, piece, rows)
    level_out(out_ref, 2 * coils * 3 * piece)


def rows_kernel(
    arrived_ref, measured_ref, keep_ref, forward_ref, inverse_ref, twiddle_ref, out_ref
):
    groups, _, rows = arrived_ref.shape
    vectors = measured_ref.shape[1]
    height = groups * rows
    inner = height // 4
    copies = vectors // keep_ref.shape[0]
    scales = [jnp.exp2(arrived_ref[g, 2 * vectors : 2 * vectors + 1, :]) for g in range(groups)]
    whole = [
        jnp.concatenate(
            [
                arrived_ref[g, part * vectors : (part + 1) * vectors, :] * scales[g]
                for g in range(groups)
            ],
            axis=1,
        )
        for part in range(2)
    ]
    a0, a1, a2, a3 = [
        (whole[0][:, n * inner : (n + 1) * inner], whole[1][:, n * inner : (n + 1) * inner])
        for n in range(4)
    ]
    even = (a0[0] + a2[0], a0[1] + a2[1])
    odd = (a0[0] - a2[0], a0[1] - a2[1])
    even_next = (a1[0] + a3[0], a1[1] + a3[1])
    odd_next = (a1[0] - a3[0], a1[1] - a3[1])
    bins = (
        (even[0] + even_next[0], even[1] + even_next[1]),
        (odd[0] + odd_next[1], odd[1] - odd_next[0]),
        (even[0] - even_next[0], even[1] - even_next[1]),
        (odd[0] - odd_next[1], odd[1] + odd_next[0]),
    )
    turned_back = []
    for index in range(4):
        turned = turn(bins[index], twiddle_ref, index, -1.0)
        spectrum = jnp.dot(
            split_pair(turned[0], turned[1], 1),
            forward_ref[...],
            preferred_element_type=jnp.float32,
        )
        lanes = slice(index * inner, (index + 1) * inner)
        keep = jnp.concatenate([keep_ref[:, lanes]] * copies, axis=0)
        residual = [
            keep * (spectrum[:, part * inner : (part + 1) * inner] - measured_ref[part, :, lanes])
            for part in range(2)
        ]
        inverse = jnp.dot(
            split_pair(residual[0], residual[1], 1),
            inverse_ref[...],
            preferred_element_type=jnp.float32,
        )
        turned_back.append(turn((inverse[:, :inner], inverse[:, inner:]), twiddle_ref, index, 1.0))
    c0, c1, c2, c3 = turned_back
    even = (c0[0] + c2[0], c0[1] + c2[1])
    odd = (c0[0] - c2[0], c0[1] - c2[1])
    even_next = (c1[0] + c3[0], c1[1] + c3[1])
    odd_next = (c1[0] - c3[0], c1[1] - c3[1])
    blocks = (
        (even[0] + even_next[0], even[1] + even_next[1]),
        (odd[0] - odd_next[1], odd[1] + odd_next[0]),
        (even[0] - even_next[0], even[1] - even_next[1]),
        (odd[0] + odd_next[1], odd[1] - odd_next[0]),
    )
    per_block = inner // rows
    for g in range(groups):
        lanes = slice((g % per_block) * rows, (g % per_block + 1) * rows)
        for part in range(2):
            out_ref[g, part * vectors : (part + 1) * vectors, :] = blocks[g // per_block][part][
                :, lanes
            ]
    level_out(out_ref, 2 * vectors)


def combine_kernel(arrived_ref, maps_ref, matrix_ref, twiddle_ref, out_ref):
    coils, _, rows, full = maps_ref.shape
    groups = arrived_ref.shape[0]
    inner = full // 3
    piece = inner // groups
    body_rows = 2 * coils * 3 * piece
    root = math.sqrt(0.75)
    scales = [jnp.exp2(arrived_ref[g, body_rows : body_rows + 1, :]) for g in range(groups)]

    def plane(part, coil, index):
        base = ((part * coils + coil) * 3 + index) * piece
        return jnp.concatenate(
            [arrived_ref[g, base : base + piece, :] * scales[g] for g in range(groups)], axis=0
        )

    turned = []
    for index in range(3):
        parts = [
            jnp.concatenate([plane(part, coil, index) for coil in range(coils)], axis=1)
            for part in range(2)
        ]
        result = lax.dot_general(
            split_pair(parts[0], parts[1], 0),
            matrix_ref[...],
            (((0,), (0,)), ((), ())),
            preferred_element_type=jnp.float32,
        )
        turned.append(turn((result[:, :inner], result[:, inner:]), twiddle_ref, index, 1.0))
    c0, c1, c2 = turned
    total = (c1[0] + c2[0], c1[1] + c2[1])
    apart = (root * (c1[0] - c2[0]), root * (c1[1] - c2[1]))
    middle = (c0[0] - 0.5 * total[0], c0[1] - 0.5 * total[1])
    blocks = (
        (c0[0] + total[0], c0[1] + total[1]),
        (middle[0] - apart[1], middle[1] + apart[0]),
        (middle[0] + apart[1], middle[1] - apart[0]),
    )
    for n in range(3):
        lanes = slice(n * inner, (n + 1) * inner)
        real = imag = None
        for coil in range(coils):
            back = [blocks[n][part][coil * rows : (coil + 1) * rows] for part in range(2)]
            map_real = maps_ref[coil, 0, :, lanes]
            map_imag = maps_ref[coil, 1, :, lanes]
            term_real = map_real * back[0] + map_imag * back[1]
            term_imag = map_real * back[1] - map_imag * back[0]
            real = term_real if real is None else real + term_real
            imag = term_imag if imag is None else imag + term_imag
        out_ref[0, :, lanes] = real
        out_ref[1, :, lanes] = imag


def call_whole(kernel, shape, name, *operands):
    return pl.pallas_call(
        kernel,
        out_shape=jax.ShapeDtypeStruct(shape, jnp.float32),
        in_specs=[pl.BlockSpec(memory_space=pltpu.VMEM)] * len(operands),
        out_specs=pl.BlockSpec(memory_space=pltpu.VMEM),
        compiler_params=pltpu.CompilerParams(vmem_limit_bytes=50 * 1024 * 1024),
        name=name,
    )(*operands)


def exchange(values):
    moved = lax.all_to_all(
        values.astype(jnp.float16), "gz", split_axis=0, concat_axis=0, tiled=True
    )
    return moved.astype(jnp.float32)


def aligned_gradient(clean_wide, coil_maps, measured, sampled):
    coils, _, rows, full = coil_maps.shape
    groups = lax.axis_size("gz")
    height = rows * groups
    inner = full // 3
    piece = inner // groups
    vectors = coils * 3 * piece
    sent = (groups, 2 * vectors + 16, rows)
    high, low = pair_matrix(inner, full, False)
    left = np.concatenate([high, high, low], axis=1)
    right = np.concatenate([high, high, low], axis=0)
    columns_twiddles = twiddle_rows(3, inner)
    spectra = call_whole(
        columns_kernel, sent, "columns", clean_wide, coil_maps, left, columns_twiddles
    )
    measured, sampled, spectra = lax.optimization_barrier((measured, sampled, spectra))
    arrived = exchange(spectra)
    place = jnp.arange(height)
    source = place // (height // 4) + 4 * (place % (height // 4))
    permute = (place[:, None] == source[None, :]).astype(jnp.float32)
    targets = jnp.transpose(measured.reshape(2, piece, 3, coils, height), (0, 3, 2, 1, 4))
    targets = jnp.dot(
        targets.reshape(2 * vectors, height), permute, precision=lax.Precision.HIGH
    ).reshape(2, vectors, height)
    keep = jnp.transpose(sampled.reshape(piece, 3, height), (1, 0, 2)).astype(jnp.bfloat16)
    keep = jnp.dot(
        keep.reshape(3 * piece, height),
        permute.astype(jnp.bfloat16),
        preferred_element_type=jnp.float32,
    )
    rows_high, rows_low = pair_matrix(height // 4, height, True)
    back_high, back_low = pair_matrix(height // 4, height, False)
    residual = call_whole(
        rows_kernel,
        sent,
        "rows",
        arrived,
        targets,
        keep,
        np.concatenate([rows_high, rows_high, rows_low], axis=0),
        np.concatenate([back_high, back_high, back_low], axis=0),
        twiddle_rows(4, height // 4),
    )
    arrived = exchange(residual)
    return call_whole(
        combine_kernel, (2, rows, full), "combine", arrived, coil_maps, right, columns_twiddles
    )


def gradient(clean_wide, coil_maps, measured, sampled):
    coils, _, rows, full = coil_maps.shape
    groups = lax.axis_size("gz")
    whole = rows % 128 == 0 and coils % 2 == 0 and full % 768 == 0
    if whole and (rows * groups) % 1024 == 0 and full % (48 * groups) == 0:
        return aligned_gradient(clean_wide, coil_maps, measured, sampled)
    return plain_gradient(clean_wide, coil_maps, measured, sampled)


def plain_gradient(clean_wide, coil_maps, measured, sampled):
    maps_real = coil_maps[:, 0]
    maps_imag = coil_maps[:, 1]
    coil_count, row_count, full_cols = maps_real.shape
    coil_pair = complex_mul((maps_real, maps_imag), (clean_wide[0][None], clean_wide[1][None]))
    spectra = transform_last(
        (
            coil_pair[0].reshape(coil_count * row_count, full_cols),
            coil_pair[1].reshape(coil_count * row_count, full_cols),
        ),
        W_FAC,
        -1.0,
    )
    groups = lax.axis_size("gz")
    pencil = full_cols // groups
    arrived = (
        lax.all_to_all(
            spectra[0].reshape(groups, pencil, coil_count, row_count),
            "gz",
            split_axis=0,
            concat_axis=3,
            tiled=True,
        ),
        lax.all_to_all(
            spectra[1].reshape(groups, pencil, coil_count, row_count),
            "gz",
            split_axis=0,
            concat_axis=3,
            tiled=True,
        ),
    )
    item_count = arrived[0].shape[2]
    height = arrived[0].shape[3]
    flattened = (
        arrived[0].reshape(pencil * item_count, height),
        arrived[1].reshape(pencil * item_count, height),
    )
    transformed = transform_last(flattened, H_FAC, -1.0)
    keeping = sampled.astype(jnp.float32)[:, None, :]
    resid_real = keeping * (transformed[0].T.reshape(pencil, item_count, height) - measured[0])
    resid_imag = keeping * (transformed[1].T.reshape(pencil, item_count, height) - measured[1])
    height = resid_real.shape[2]
    inverse = transform_last(
        (
            resid_real.reshape(pencil * coil_count, height),
            resid_imag.reshape(pencil * coil_count, height),
        ),
        H_FAC,
        1.0,
    )
    arrived = (
        lax.all_to_all(
            inverse[0].T.reshape(pencil, coil_count, groups, row_count),
            "gz",
            split_axis=2,
            concat_axis=0,
            tiled=True,
        ),
        lax.all_to_all(
            inverse[1].T.reshape(pencil, coil_count, groups, row_count),
            "gz",
            split_axis=2,
            concat_axis=0,
            tiled=True,
        ),
    )
    item_count = arrived[0].shape[1]
    flattened = (
        arrived[0].reshape(full_cols, item_count * row_count),
        arrived[1].reshape(full_cols, item_count * row_count),
    )
    transformed = transform_first(flattened, W_FAC, 1.0)
    back_real = jnp.transpose(transformed[0].reshape(full_cols, item_count, row_count), (1, 2, 0))
    back_imag = jnp.transpose(transformed[1].reshape(full_cols, item_count, row_count), (1, 2, 0))
    grad_real = jnp.sum(maps_real * back_real + maps_imag * back_imag, axis=0)
    grad_imag = jnp.sum(maps_real * back_imag - maps_imag * back_real, axis=0)
    return jnp.stack([grad_real, grad_imag])


def local(
    noisy_image, fresh_noise, coil_maps, measured, sampled, first_kernel, inner_kernels, last_kernel
):
    predicted = network(noisy_image, first_kernel, inner_kernels, last_kernel)
    clean = (noisy_image - SIGMA_NOW * predicted) / SCALE_NOW
    clean_wide = lax.all_gather(clean, "col", axis=2, tiled=True)
    grad = gradient(clean_wide, coil_maps, measured, sampled)
    grad_tile = lax.psum_scatter(
        grad, "col", scatter_dimension=2, tiled=True
    )
    update = clean - STEP_GAIN * grad_tile
    return SCALE_NEXT * update + DIRECT_GAIN * predicted + NOISE_GAIN * fresh_noise


def solution(mesh):
    in_specs = (
        P("grp", "gz", "col"),
        P("grp", "gz", "col"),
        P("col", "grp", "gz", None),
        P("grp", "gz", "col", None),
        P("gz", "grp"),
        P(),
        P(),
        P(),
    )
    out_specs = P("grp", "gz", "col")
    return jax.shard_map(local, mesh=mesh, in_specs=in_specs, out_specs=out_specs, check_vma=False)
```

```python
from functools import partial
import math

import jax
import jax.numpy as jnp
import numpy as np
from jax import lax
from jax.experimental import pallas as pl
from jax.experimental.pallas import tpu as pltpu
from jax.sharding import PartitionSpec as P

H_FAC = 8
W_FAC = 6
ROWS = 4


SCALE_NOW = 0.8
SIGMA_NOW = 0.6
STEP_GAIN = 1.0
SCALE_NEXT = 0.9
DIRECT_GAIN = 0.31622776601683794
NOISE_GAIN = 0.3


def with_halo(block, sides, width):
    for axis, dim in sides:
        count = lax.axis_size(axis)
        forward = [(i, i + 1) for i in range(count - 1)]
        backward = [(target, source) for source, target in forward]
        low = lax.ppermute(
            lax.slice_in_dim(block, block.shape[dim] - width, None, axis=dim), axis, forward
        )
        high = lax.ppermute(lax.slice_in_dim(block, 0, width, axis=dim), axis, backward)
        block = jnp.concatenate([low, block, high], axis=dim)
    return block


def row_banded(kernel, span):
    taps = kernel.reshape(3, 3, kernel.shape[1], kernel.shape[2])
    return jnp.stack(
        [
            jnp.pad(taps, ((start, span - 3 - start), (0, 0), (0, 0), (0, 0)))
            for start in range(span - 2)
        ]
    )


def network_kernel(
    groups,
    cols,
    tiles_ref,
    first_ref,
    inner_ref,
    last_ref,
    first_rows_ref,
    inner_rows_ref,
    inside_ref,
    out_ref,
    first_held,
    inner_held,
):
    frame, width = inside_ref.shape
    half = width // 2

    def act(halved, keep):
        return (halved + halved * jnp.tanh(halved)) * (inside_ref[...] * keep)

    def first_layer(group):
        halved = jnp.dot(
            tiles_ref[group // ROWS],
            first_ref[lax.rem(group, ROWS)],
            preferred_element_type=jnp.float32,
        )
        hidden = act(halved, first_rows_ref[group])
        slot = lax.rem(group, ROWS)
        first_held[slot, 0] = pltpu.roll(hidden, 1, 0).astype(jnp.bfloat16)
        first_held[slot, 1] = hidden.astype(jnp.bfloat16)
        first_held[slot, 2] = pltpu.roll(hidden, frame - 1, 0).astype(jnp.bfloat16)

    def inner_layer(group):
        slot = lax.rem(group, ROWS)
        after = lax.rem(group + 1, ROWS)
        total = None
        for shift in range(3):
            part = jnp.dot(
                first_held[slot, shift],
                inner_ref[shift, :width],
                preferred_element_type=jnp.float32,
            ) + jnp.dot(
                first_held[after, shift, :, :half],
                inner_ref[shift, width:],
                preferred_element_type=jnp.float32,
            )
            total = part if total is None else total + part
        inner_held[slot] = act(total, inner_rows_ref[group]).astype(jnp.bfloat16)

    def last_layer(group):
        slot = lax.rem(group, ROWS)
        after = lax.rem(group + 1, ROWS)
        lanes = (((1,), (1,)), ((), ()))
        part = lax.dot_general(
            last_ref[:, :width], inner_held[slot], lanes, preferred_element_type=jnp.float32
        ) + lax.dot_general(
            last_ref[:, width:],
            inner_held[after, :, :half],
            lanes,
            preferred_element_type=jnp.float32,
        )
        left = part[:8]
        left = jnp.concatenate([left[:, frame - 1 :], left[:, : cols - 1]], axis=1)
        out_ref[group] = left + part[8:16, :cols] + part[16:24, 1 : cols + 1]

    for group in range(4):
        first_layer(group)
    for group in range(2):
        inner_layer(group)

    def step(group, carry):
        last_layer(group)
        inner_layer(group + 2)
        first_layer(group + 4)
        return carry

    lax.fori_loop(0, groups, step, 0)


def network(image, first_kernel, inner_kernels, last_kernel):
    channels, rows, cols = image.shape
    hidden = first_kernel.shape[1]
    groups = rows // ROWS
    frame = cols + 16
    width = ROWS * hidden
    span = ROWS * ROWS + 2
    tile_count = groups // ROWS + 1
    padded = with_halo(image.astype(jnp.bfloat16), (("gz", 1), ("col", 2)), 3)
    padded = jnp.pad(padded, ((0, 0), (0, ROWS * ROWS * tile_count + 2 - rows - 6), (0, 0)))
    gap = jnp.zeros(padded.shape[:2] + (frame - cols - 6,), padded.dtype)
    ring = jnp.concatenate([padded[:, :, 3:], gap, padded[:, :, :3]], axis=2)
    shifted = jnp.stack([jnp.roll(ring, 1 - shift, axis=2) for shift in range(3)])
    tiles = jnp.stack(
        [shifted[:, :, ROWS * ROWS * t : ROWS * ROWS * t + span] for t in range(tile_count)]
    )
    depth = 3 * channels * span
    tiles = jnp.transpose(tiles.reshape(tile_count, depth, frame), (0, 2, 1))
    tiles = jnp.pad(tiles, ((0, 0), (0, 0), (0, 128 - depth)))
    half = jnp.asarray(0.5, jnp.bfloat16)
    first = jnp.transpose(row_banded(first_kernel * half, span), (2, 4, 1, 0, 3))
    first = first.reshape(depth, ROWS, width)
    first = jnp.pad(jnp.transpose(first, (1, 0, 2)), ((0, 0), (0, 128 - depth), (0, 0)))
    inner = jnp.transpose(row_banded(inner_kernels[0] * half, ROWS + 2), (2, 1, 4, 0, 3))
    inner = inner.reshape(3, (ROWS + 2) * hidden, width)
    last = jnp.transpose(row_banded(last_kernel, ROWS + 2), (2, 0, 3, 1, 4))
    last = last.reshape(3 * ROWS * channels, (ROWS + 2) * hidden)
    last = jnp.pad(last, ((0, 32 - last.shape[0]), (0, 0)))
    top = lax.axis_index("gz") * rows
    height = rows * lax.axis_size("gz")
    across = cols * lax.axis_size("col")

    def row_mask(count, offset):
        place = top + ROWS * jnp.arange(count)[:, None] + jnp.arange(ROWS)[None, :] - offset
        keep = ((place >= 0) & (place < height)).astype(jnp.float32)
        return jnp.repeat(keep, hidden, axis=1).reshape(count, 1, width)

    spot = jnp.arange(frame)
    spot = jnp.where(spot < cols + 8, spot, spot - frame) + lax.axis_index("col") * cols
    inside = ((spot >= 0) & (spot < across)).astype(jnp.float32)
    inside = jnp.broadcast_to(inside[:, None], (frame, width))
    result = pl.pallas_call(
        partial(network_kernel, groups, cols),
        out_shape=jax.ShapeDtypeStruct((groups, ROWS * channels, cols), jnp.float32),
        in_specs=[pl.BlockSpec(memory_space=pltpu.VMEM)] * 7,
        out_specs=pl.BlockSpec(memory_space=pltpu.VMEM),
        scratch_shapes=[
            pltpu.VMEM((ROWS, 3, frame, width), jnp.bfloat16),
            pltpu.VMEM((ROWS, frame, width), jnp.bfloat16),
        ],
        compiler_params=pltpu.CompilerParams(vmem_limit_bytes=40 * 1024 * 1024),
        name="network",
    )(tiles, first, inner, last, row_mask(groups + 4, 2), row_mask(groups + 2, 1), inside)
    result = result.reshape(groups, ROWS, channels, cols)
    return jnp.transpose(result, (2, 0, 1, 3)).reshape(channels, rows, cols)


def rotation(rows_len, cols_len, modulus, direction):
    first_index = jnp.arange(rows_len, dtype=jnp.int32)
    second_index = jnp.arange(cols_len, dtype=jnp.int32)
    phase_index = first_index[:, None] * second_index[None, :] % modulus
    angles = phase_index.astype(jnp.float32) * (direction * 2.0 * math.pi / modulus)
    return (jnp.cos(angles), jnp.sin(angles))


def complex_dot(matrix_pair, data_pair, contracting):
    product = partial(
        lax.dot_general,
        dimension_numbers=(contracting, ((), ())),
        precision=lax.Precision.HIGH,
        preferred_element_type=jnp.float32,
    )
    return (
        product(matrix_pair[0], data_pair[0]) - product(matrix_pair[1], data_pair[1]),
        product(matrix_pair[0], data_pair[1]) + product(matrix_pair[1], data_pair[0]),
    )


def complex_mul(first_pair, second_pair):
    return (
        first_pair[0] * second_pair[0] - first_pair[1] * second_pair[1],
        first_pair[0] * second_pair[1] + first_pair[1] * second_pair[0],
    )


def transform_last(data_pair, outer_len, direction):
    vectors, length = data_pair[0].shape
    inner_len = length // outer_len
    shaped = (
        data_pair[0].reshape(vectors, outer_len, inner_len),
        data_pair[1].reshape(vectors, outer_len, inner_len),
    )
    sectioned = complex_dot(
        rotation(outer_len, outer_len, outer_len, direction), shaped, ((1,), (1,))
    )
    twiddles = rotation(outer_len, inner_len, length, direction)
    twisted = complex_mul(sectioned, (twiddles[0][:, None, :], twiddles[1][:, None, :]))
    finished = complex_dot(
        rotation(inner_len, inner_len, inner_len, direction), twisted, ((1,), (2,))
    )
    factor = 1.0 / math.sqrt(length)
    return (
        finished[0].reshape(length, vectors) * factor,
        finished[1].reshape(length, vectors) * factor,
    )


def transform_first(data_pair, outer_len, direction):
    length, vectors = data_pair[0].shape
    inner_len = length // outer_len
    shaped = (
        data_pair[0].reshape(outer_len, inner_len, vectors),
        data_pair[1].reshape(outer_len, inner_len, vectors),
    )
    sectioned = complex_dot(
        rotation(outer_len, outer_len, outer_len, direction), shaped, ((1,), (0,))
    )
    twiddles = rotation(outer_len, inner_len, length, direction)
    twisted = complex_mul(sectioned, (twiddles[0][:, :, None], twiddles[1][:, :, None]))
    finished = complex_dot(
        rotation(inner_len, inner_len, inner_len, direction), twisted, ((1,), (1,))
    )
    factor = 1.0 / math.sqrt(length)
    return (
        finished[0].reshape(length, vectors) * factor,
        finished[1].reshape(length, vectors) * factor,
    )


def split_pair(real, imag, axis):
    both = jnp.concatenate([real, imag], axis=axis)
    high = both.astype(jnp.bfloat16)
    low = (both - high.astype(jnp.float32)).astype(jnp.bfloat16)
    return jnp.concatenate([high, low, high], axis=axis)


def pair_matrix(inner, length, transposed):
    angles = np.outer(np.arange(inner), np.arange(inner)) % inner * (2.0 * np.pi / inner)
    cosines, sines = np.cos(angles), np.sin(angles)
    matrix = np.block([[cosines, sines], [-sines, cosines]]) / np.sqrt(length)
    if transposed:
        matrix = matrix.T
    high = matrix.astype(jnp.bfloat16)
    low = (matrix - high.astype(np.float64)).astype(jnp.bfloat16)
    return high, low


def twiddle_rows(outer, inner):
    angles = np.outer(np.arange(outer), np.arange(inner)) * (2.0 * np.pi / (outer * inner))
    return np.stack([np.cos(angles), np.sin(angles)], axis=1).astype(np.float32)


def turn(pair, twiddle_ref, index, sign):
    if index == 0:
        return pair
    cosine = twiddle_ref[index, 0:1]
    sine = sign * twiddle_ref[index, 1:2]
    return (pair[0] * cosine - pair[1] * sine, pair[0] * sine + pair[1] * cosine)


def level_out(out_ref, body_rows):
    values = out_ref[:, :body_rows, :]
    top = jnp.max(jnp.max(jnp.abs(values), axis=0), axis=0, keepdims=True)
    top = jnp.maximum(jnp.max(top, axis=1, keepdims=True), 1e-30)
    power = jnp.ceil(jnp.log2(top)) - 13.0
    out_ref[:, :body_rows, :] = values * jnp.exp2(-power)
    tail = out_ref.shape[1] - body_rows
    out_ref[:, body_rows:, :] = jnp.broadcast_to(
        power[None], (out_ref.shape[0], tail, out_ref.shape[2])
    )


def columns_kernel(clean_ref, maps_ref, matrix_ref, twiddle_ref, out_ref):
    coils, _, rows, full = maps_ref.shape
    groups = out_ref.shape[0]
    inner = full // 3
    piece = inner // groups
    root = math.sqrt(0.75)
    clean = (clean_ref[0], clean_ref[1])
    for start in range(0, coils, 2):
        image = [
            complex_mul((maps_ref[coil, 0], maps_ref[coil, 1]), clean)
            for coil in (start, start + 1)
        ]
        image = [jnp.concatenate([image[0][part], image[1][part]], axis=0) for part in range(2)]
        first, second, third = [
            (image[0][:, n * inner : (n + 1) * inner], image[1][:, n * inner : (n + 1) * inner])
            for n in range(3)
        ]
        total = (second[0] + third[0], second[1] + third[1])
        apart = (root * (second[0] - third[0]), root * (second[1] - third[1]))
        middle = (first[0] - 0.5 * total[0], first[1] - 0.5 * total[1])
        bins = (
            (first[0] + total[0], first[1] + total[1]),
            (middle[0] + apart[1], middle[1] - apart[0]),
            (middle[0] - apart[1], middle[1] + apart[0]),
        )
        for index in range(3):
            turned = turn(bins[index], twiddle_ref, index, -1.0)
            result = lax.dot_general(
                matrix_ref[...],
                split_pair(turned[0], turned[1], 1),
                (((1,), (1,)), ((), ())),
                preferred_element_type=jnp.float32,
            )
            for part in range(2):
                for which in range(2):
                    base = ((part * coils + start + which) * 3 + index) * piece
                    block = result[part * inner : (part + 1) * inner]
                    block = block[:, which * rows : (which + 1) * rows]
                    out_ref[:, base : base + piece, :] = block.reshape(groups, piece, rows)
    level_out(out_ref, 2 * coils * 3 * piece)


def rows_kernel(
    arrived_ref, measured_ref, keep_ref, forward_ref, inverse_ref, twiddle_ref, out_ref
):
    groups, _, rows = arrived_ref.shape
    vectors = measured_ref.shape[1]
    height = groups * rows
    inner = height // 4
    copies = vectors // keep_ref.shape[0]
    scales = [jnp.exp2(arrived_ref[g, 2 * vectors : 2 * vectors + 1, :]) for g in range(groups)]
    whole = [
        jnp.concatenate(
            [
                arrived_ref[g, part * vectors : (part + 1) * vectors, :] * scales[g]
                for g in range(groups)
            ],
            axis=1,
        )
        for part in range(2)
    ]
    a0, a1, a2, a3 = [
        (whole[0][:, n * inner : (n + 1) * inner], whole[1][:, n * inner : (n + 1) * inner])
        for n in range(4)
    ]
    even = (a0[0] + a2[0], a0[1] + a2[1])
    odd = (a0[0] - a2[0], a0[1] - a2[1])
    even_next = (a1[0] + a3[0], a1[1] + a3[1])
    odd_next = (a1[0] - a3[0], a1[1] - a3[1])
    bins = (
        (even[0] + even_next[0], even[1] + even_next[1]),
        (odd[0] + odd_next[1], odd[1] - odd_next[0]),
        (even[0] - even_next[0], even[1] - even_next[1]),
        (odd[0] - odd_next[1], odd[1] + odd_next[0]),
    )
    turned_back = []
    for index in range(4):
        turned = turn(bins[index], twiddle_ref, index, -1.0)
        spectrum = jnp.dot(
            split_pair(turned[0], turned[1], 1),
            forward_ref[...],
            preferred_element_type=jnp.float32,
        )
        lanes = slice(index * inner, (index + 1) * inner)
        keep = jnp.concatenate([keep_ref[:, lanes]] * copies, axis=0)
        residual = [
            keep * (spectrum[:, part * inner : (part + 1) * inner] - measured_ref[part, :, lanes])
            for part in range(2)
        ]
        inverse = jnp.dot(
            split_pair(residual[0], residual[1], 1),
            inverse_ref[...],
            preferred_element_type=jnp.float32,
        )
        turned_back.append(turn((inverse[:, :inner], inverse[:, inner:]), twiddle_ref, index, 1.0))
    c0, c1, c2, c3 = turned_back
    even = (c0[0] + c2[0], c0[1] + c2[1])
    odd = (c0[0] - c2[0], c0[1] - c2[1])
    even_next = (c1[0] + c3[0], c1[1] + c3[1])
    odd_next = (c1[0] - c3[0], c1[1] - c3[1])
    blocks = (
        (even[0] + even_next[0], even[1] + even_next[1]),
        (odd[0] - odd_next[1], odd[1] + odd_next[0]),
        (even[0] - even_next[0], even[1] - even_next[1]),
        (odd[0] + odd_next[1], odd[1] - odd_next[0]),
    )
    per_block = inner // rows
    for g in range(groups):
        lanes = slice((g % per_block) * rows, (g % per_block + 1) * rows)
        for part in range(2):
            out_ref[g, part * vectors : (part + 1) * vectors, :] = blocks[g // per_block][part][
                :, lanes
            ]
    level_out(out_ref, 2 * vectors)


def combine_kernel(arrived_ref, maps_ref, matrix_ref, twiddle_ref, *refs):
    earlier_ref, out_ref = refs if len(refs) == 2 else (None, refs[0])
    coils, _, rows, full = maps_ref.shape
    groups = arrived_ref.shape[0]
    inner = full // 3
    piece = inner // groups
    body_rows = 2 * coils * 3 * piece
    root = math.sqrt(0.75)
    scales = [jnp.exp2(arrived_ref[g, body_rows : body_rows + 1, :]) for g in range(groups)]

    def plane(part, coil, index):
        base = ((part * coils + coil) * 3 + index) * piece
        return jnp.concatenate(
            [arrived_ref[g, base : base + piece, :] * scales[g] for g in range(groups)], axis=0
        )

    turned = []
    for index in range(3):
        parts = [
            jnp.concatenate([plane(part, coil, index) for coil in range(coils)], axis=1)
            for part in range(2)
        ]
        result = lax.dot_general(
            split_pair(parts[0], parts[1], 0),
            matrix_ref[...],
            (((0,), (0,)), ((), ())),
            preferred_element_type=jnp.float32,
        )
        turned.append(turn((result[:, :inner], result[:, inner:]), twiddle_ref, index, 1.0))
    c0, c1, c2 = turned
    total = (c1[0] + c2[0], c1[1] + c2[1])
    apart = (root * (c1[0] - c2[0]), root * (c1[1] - c2[1]))
    middle = (c0[0] - 0.5 * total[0], c0[1] - 0.5 * total[1])
    blocks = (
        (c0[0] + total[0], c0[1] + total[1]),
        (middle[0] - apart[1], middle[1] + apart[0]),
        (middle[0] + apart[1], middle[1] - apart[0]),
    )
    share = out_ref.shape[3]
    for start in range(0, full, 128):
        n, inside = start // inner, slice(start % inner, start % inner + 128)
        lanes = slice(start, start + 128)
        half, place = start // share, slice(start % share, start % share + 128)
        real = 0.0 if earlier_ref is None else earlier_ref[half, 0, :, place]
        imag = 0.0 if earlier_ref is None else earlier_ref[half, 1, :, place]
        for coil in range(coils):
            back = [
                blocks[n][part][coil * rows : (coil + 1) * rows, inside] for part in range(2)
            ]
            map_real = maps_ref[coil, 0, :, lanes]
            map_imag = maps_ref[coil, 1, :, lanes]
            real = real + map_real * back[0] + map_imag * back[1]
            imag = imag + map_real * back[1] - map_imag * back[0]
        out_ref[half, 0, :, place] = real
        out_ref[half, 1, :, place] = imag


def whole_block(operand):
    return pl.BlockSpec(operand.shape, lambda i: (0,) * operand.ndim)


def part_block(operand, axis, parts, index):
    block = list(operand.shape)
    block[axis] //= parts
    return pl.BlockSpec(
        tuple(block), lambda i: tuple(index if a == axis else 0 for a in range(operand.ndim))
    )


def call_whole(kernel, shape, name, flops, *operands, specs=None):
    specs = specs or {}
    return pl.pallas_call(
        kernel,
        grid=(1,),
        out_shape=jax.ShapeDtypeStruct(shape, jnp.float32),
        in_specs=[specs.get(i) or whole_block(operand) for i, operand in enumerate(operands)],
        out_specs=pl.BlockSpec(shape, lambda i: (0,) * len(shape)),
        compiler_params=pltpu.CompilerParams(vmem_limit_bytes=50 * 1024 * 1024),
        cost_estimate=pl.CostEstimate(
            flops=flops, bytes_accessed=8 * math.prod(shape), transcendentals=0
        ),
        name=name,
    )(*operands)


def exchange(values):
    moved = lax.all_to_all(
        values.astype(jnp.float16), "gz", split_axis=0, concat_axis=0, tiled=True
    )
    return moved.astype(jnp.float32)


def aligned_gradient(clean_wide, coil_maps, measured, sampled):
    coils, _, rows, full = coil_maps.shape
    groups = lax.axis_size("gz")
    height = rows * groups
    inner = full // 3
    piece = inner // groups
    parts = 2
    vectors = coils // parts * 3 * piece
    sent = (groups, 2 * vectors + 16, rows)
    flops = 12 * vectors * inner * rows * groups
    high, low = pair_matrix(inner, full, False)
    left = np.concatenate([high, high, low], axis=1)
    right = np.concatenate([high, high, low], axis=0)
    columns_twiddles = twiddle_rows(3, inner)
    rows_high, rows_low = pair_matrix(height // 4, height, True)
    back_high, back_low = pair_matrix(height // 4, height, False)
    forward = np.concatenate([rows_high, rows_high, rows_low], axis=0)
    inverse = np.concatenate([back_high, back_high, back_low], axis=0)
    rows_twiddles = twiddle_rows(4, height // 4)
    spectra = []
    for part in range(parts):
        maps = {1: part_block(coil_maps, 0, parts, part)}
        operands = (clean_wide, coil_maps, left, columns_twiddles)
        spectra.append(
            call_whole(columns_kernel, sent, "columns", flops, *operands, specs=maps)
        )
        if part == 0:
            measured, sampled, spectra[0] = lax.optimization_barrier(
                (measured, sampled, spectra[0])
            )
    arrived = [exchange(values) for values in spectra]
    arrived[0], spectra[1] = lax.optimization_barrier((arrived[0], spectra[1]))
    place = jnp.arange(height)
    source = place // (height // 4) + 4 * (place % (height // 4))
    permute = (place[:, None] == source[None, :]).astype(jnp.float32)
    targets = jnp.transpose(measured.reshape(2, piece, 3, coils, height), (0, 3, 2, 1, 4))
    targets = jnp.dot(
        targets.reshape(2 * parts * vectors, height), permute, precision=lax.Precision.HIGH
    ).reshape(2, parts * vectors, height)
    keep = jnp.transpose(sampled.reshape(piece, 3, height), (1, 0, 2)).astype(jnp.bfloat16)
    keep = jnp.dot(
        keep.reshape(3 * piece, height),
        permute.astype(jnp.bfloat16),
        preferred_element_type=jnp.float32,
    )
    residual = []
    for part in range(parts):
        target = {1: part_block(targets, 1, parts, part)}
        operands = (arrived[part], targets, keep, forward, inverse, rows_twiddles)
        residual.append(
            call_whole(rows_kernel, sent, "rows", 2 * flops, *operands, specs=target)
        )
    arrived = [exchange(values) for values in residual]
    arrived[0], residual[1] = lax.optimization_barrier((arrived[0], residual[1]))
    halves = lax.axis_size("col")
    total = ()
    for part in range(parts):
        maps = {1: part_block(coil_maps, 0, parts, part)}
        operands = (arrived[part], coil_maps, right, columns_twiddles) + total
        shape = (halves, 2, rows, full // halves)
        total = (call_whole(combine_kernel, shape, "combine", flops, *operands, specs=maps),)
    return total[0]


def gradient(clean_wide, coil_maps, measured, sampled):
    coils, _, rows, full = coil_maps.shape
    groups = lax.axis_size("gz")
    whole = rows % 128 == 0 and coils % 4 == 0 and full % 768 == 0
    if whole and (rows * groups) % 1024 == 0 and full % (48 * groups) == 0:
        return aligned_gradient(clean_wide, coil_maps, measured, sampled)
    grad = plain_gradient(clean_wide, coil_maps, measured, sampled)
    return jnp.stack(jnp.split(grad, lax.axis_size("col"), axis=2))


def plain_gradient(clean_wide, coil_maps, measured, sampled):
    maps_real = coil_maps[:, 0]
    maps_imag = coil_maps[:, 1]
    coil_count, row_count, full_cols = maps_real.shape
    coil_pair = complex_mul((maps_real, maps_imag), (clean_wide[0][None], clean_wide[1][None]))
    spectra = transform_last(
        (
            coil_pair[0].reshape(coil_count * row_count, full_cols),
            coil_pair[1].reshape(coil_count * row_count, full_cols),
        ),
        W_FAC,
        -1.0,
    )
    groups = lax.axis_size("gz")
    pencil = full_cols // groups
    arrived = (
        lax.all_to_all(
            spectra[0].reshape(groups, pencil, coil_count, row_count),
            "gz",
            split_axis=0,
            concat_axis=3,
            tiled=True,
        ),
        lax.all_to_all(
            spectra[1].reshape(groups, pencil, coil_count, row_count),
            "gz",
            split_axis=0,
            concat_axis=3,
            tiled=True,
        ),
    )
    item_count = arrived[0].shape[2]
    height = arrived[0].shape[3]
    flattened = (
        arrived[0].reshape(pencil * item_count, height),
        arrived[1].reshape(pencil * item_count, height),
    )
    transformed = transform_last(flattened, H_FAC, -1.0)
    keeping = sampled.astype(jnp.float32)[:, None, :]
    resid_real = keeping * (transformed[0].T.reshape(pencil, item_count, height) - measured[0])
    resid_imag = keeping * (transformed[1].T.reshape(pencil, item_count, height) - measured[1])
    height = resid_real.shape[2]
    inverse = transform_last(
        (
            resid_real.reshape(pencil * coil_count, height),
            resid_imag.reshape(pencil * coil_count, height),
        ),
        H_FAC,
        1.0,
    )
    arrived = (
        lax.all_to_all(
            inverse[0].T.reshape(pencil, coil_count, groups, row_count),
            "gz",
            split_axis=2,
            concat_axis=0,
            tiled=True,
        ),
        lax.all_to_all(
            inverse[1].T.reshape(pencil, coil_count, groups, row_count),
            "gz",
            split_axis=2,
            concat_axis=0,
            tiled=True,
        ),
    )
    item_count = arrived[0].shape[1]
    flattened = (
        arrived[0].reshape(full_cols, item_count * row_count),
        arrived[1].reshape(full_cols, item_count * row_count),
    )
    transformed = transform_first(flattened, W_FAC, 1.0)
    back_real = jnp.transpose(transformed[0].reshape(full_cols, item_count, row_count), (1, 2, 0))
    back_imag = jnp.transpose(transformed[1].reshape(full_cols, item_count, row_count), (1, 2, 0))
    grad_real = jnp.sum(maps_real * back_real + maps_imag * back_imag, axis=0)
    grad_imag = jnp.sum(maps_real * back_imag - maps_imag * back_real, axis=0)
    return jnp.stack([grad_real, grad_imag])


def local(
    noisy_image, fresh_noise, coil_maps, measured, sampled, first_kernel, inner_kernels, last_kernel
):
    predicted = network(noisy_image, first_kernel, inner_kernels, last_kernel)
    clean = (noisy_image - SIGMA_NOW * predicted) / SCALE_NOW
    clean_wide = lax.all_gather(clean, "col", axis=2, tiled=True)
    grad = gradient(clean_wide, coil_maps, measured, sampled)
    if lax.axis_size("col") == 2:
        here = lax.axis_index("col")
        away = lax.dynamic_index_in_dim(grad, 1 - here, 0, keepdims=False)
        grad_tile = lax.dynamic_index_in_dim(grad, here, 0, keepdims=False)
        grad_tile = grad_tile + lax.ppermute(away, "col", [(0, 1), (1, 0)])
    else:
        grad_tile = lax.psum_scatter(grad, "col", scatter_dimension=0, tiled=False)
    update = clean - STEP_GAIN * grad_tile
    return SCALE_NEXT * update + DIRECT_GAIN * predicted + NOISE_GAIN * fresh_noise


def solution(mesh):
    in_specs = (
        P("grp", "gz", "col"),
        P("grp", "gz", "col"),
        P("col", "grp", "gz", None),
        P("grp", "gz", "col", None),
        P("gz", "grp"),
        P(),
        P(),
        P(),
    )
    out_specs = P("grp", "gz", "col")
    return jax.shard_map(local, mesh=mesh, in_specs=in_specs, out_specs=out_specs, check_vma=False)
```

```python
from functools import partial
import math

import jax
import jax.numpy as jnp
import numpy as np
from jax import lax
from jax.experimental import pallas as pl
from jax.experimental.pallas import tpu as pltpu
from jax.sharding import PartitionSpec as P

H_FAC = 8
W_FAC = 6
ROWS = 4
PIECE = 32


SCALE_NOW = 0.8
SIGMA_NOW = 0.6
STEP_GAIN = 1.0
SCALE_NEXT = 0.9
DIRECT_GAIN = 0.31622776601683794
NOISE_GAIN = 0.3


def with_halo(block, sides, width):
    for axis, dim in sides:
        count = lax.axis_size(axis)
        forward = [(i, i + 1) for i in range(count - 1)]
        backward = [(target, source) for source, target in forward]
        low = lax.ppermute(
            lax.slice_in_dim(block, block.shape[dim] - width, None, axis=dim), axis, forward
        )
        high = lax.ppermute(lax.slice_in_dim(block, 0, width, axis=dim), axis, backward)
        block = jnp.concatenate([low, block, high], axis=dim)
    return block


def row_banded(kernel, span):
    taps = kernel.reshape(3, 3, kernel.shape[1], kernel.shape[2])
    return jnp.stack(
        [
            jnp.pad(taps, ((start, span - 3 - start), (0, 0), (0, 0), (0, 0)))
            for start in range(span - 2)
        ]
    )


def network_kernel(
    groups,
    cols,
    tiles_ref,
    first_ref,
    inner_ref,
    last_ref,
    first_rows_ref,
    inner_rows_ref,
    inside_ref,
    out_ref,
    first_held,
    inner_held,
):
    frame, width = inside_ref.shape
    half = width // 2

    def act(halved, keep):
        return (halved + halved * jnp.tanh(halved)) * (inside_ref[...] * keep)

    def first_layer(group):
        halved = jnp.dot(
            tiles_ref[group // ROWS],
            first_ref[lax.rem(group, ROWS)],
            preferred_element_type=jnp.float32,
        )
        hidden = act(halved, first_rows_ref[group])
        slot = lax.rem(group, ROWS)
        first_held[slot, 0] = pltpu.roll(hidden, 1, 0).astype(jnp.bfloat16)
        first_held[slot, 1] = hidden.astype(jnp.bfloat16)
        first_held[slot, 2] = pltpu.roll(hidden, frame - 1, 0).astype(jnp.bfloat16)

    def inner_layer(group):
        slot = lax.rem(group, ROWS)
        after = lax.rem(group + 1, ROWS)
        total = None
        for shift in range(3):
            part = jnp.dot(
                first_held[slot, shift],
                inner_ref[shift, :width],
                preferred_element_type=jnp.float32,
            ) + jnp.dot(
                first_held[after, shift, :, :half],
                inner_ref[shift, width:],
                preferred_element_type=jnp.float32,
            )
            total = part if total is None else total + part
        inner_held[slot] = act(total, inner_rows_ref[group]).astype(jnp.bfloat16)

    def last_layer(group):
        slot = lax.rem(group, ROWS)
        after = lax.rem(group + 1, ROWS)
        lanes = (((1,), (1,)), ((), ()))
        part = lax.dot_general(
            last_ref[:, :width], inner_held[slot], lanes, preferred_element_type=jnp.float32
        ) + lax.dot_general(
            last_ref[:, width:],
            inner_held[after, :, :half],
            lanes,
            preferred_element_type=jnp.float32,
        )
        left = part[:8]
        left = jnp.concatenate([left[:, frame - 1 :], left[:, : cols - 1]], axis=1)
        out_ref[group] = left + part[8:16, :cols] + part[16:24, 1 : cols + 1]

    for group in range(4):
        first_layer(group)
    for group in range(2):
        inner_layer(group)

    def step(group, carry):
        last_layer(group)
        inner_layer(group + 2)
        first_layer(group + 4)
        return carry

    lax.fori_loop(0, groups, step, 0)


def network(image, first_kernel, inner_kernels, last_kernel):
    channels, rows, cols = image.shape
    hidden = first_kernel.shape[1]
    groups = rows // ROWS
    frame = cols + 16
    width = ROWS * hidden
    span = ROWS * ROWS + 2
    tile_count = groups // ROWS + 1
    padded = with_halo(image.astype(jnp.bfloat16), (("gz", 1), ("col", 2)), 3)
    padded = jnp.pad(padded, ((0, 0), (0, ROWS * ROWS * tile_count + 2 - rows - 6), (0, 0)))
    gap = jnp.zeros(padded.shape[:2] + (frame - cols - 6,), padded.dtype)
    ring = jnp.concatenate([padded[:, :, 3:], gap, padded[:, :, :3]], axis=2)
    shifted = jnp.stack([jnp.roll(ring, 1 - shift, axis=2) for shift in range(3)])
    tiles = jnp.stack(
        [shifted[:, :, ROWS * ROWS * t : ROWS * ROWS * t + span] for t in range(tile_count)]
    )
    depth = 3 * channels * span
    tiles = jnp.transpose(tiles.reshape(tile_count, depth, frame), (0, 2, 1))
    tiles = jnp.pad(tiles, ((0, 0), (0, 0), (0, 128 - depth)))
    half = jnp.asarray(0.5, jnp.bfloat16)
    first = jnp.transpose(row_banded(first_kernel * half, span), (2, 4, 1, 0, 3))
    first = first.reshape(depth, ROWS, width)
    first = jnp.pad(jnp.transpose(first, (1, 0, 2)), ((0, 0), (0, 128 - depth), (0, 0)))
    inner = jnp.transpose(row_banded(inner_kernels[0] * half, ROWS + 2), (2, 1, 4, 0, 3))
    inner = inner.reshape(3, (ROWS + 2) * hidden, width)
    last = jnp.transpose(row_banded(last_kernel, ROWS + 2), (2, 0, 3, 1, 4))
    last = last.reshape(3 * ROWS * channels, (ROWS + 2) * hidden)
    last = jnp.pad(last, ((0, 32 - last.shape[0]), (0, 0)))
    top = lax.axis_index("gz") * rows
    height = rows * lax.axis_size("gz")
    across = cols * lax.axis_size("col")

    def row_mask(count, offset):
        place = top + ROWS * jnp.arange(count)[:, None] + jnp.arange(ROWS)[None, :] - offset
        keep = ((place >= 0) & (place < height)).astype(jnp.float32)
        return jnp.repeat(keep, hidden, axis=1).reshape(count, 1, width)

    spot = jnp.arange(frame)
    spot = jnp.where(spot < cols + 8, spot, spot - frame) + lax.axis_index("col") * cols
    inside = ((spot >= 0) & (spot < across)).astype(jnp.float32)
    inside = jnp.broadcast_to(inside[:, None], (frame, width))
    result = pl.pallas_call(
        partial(network_kernel, groups, cols),
        out_shape=jax.ShapeDtypeStruct((groups, ROWS * channels, cols), jnp.float32),
        in_specs=[pl.BlockSpec(memory_space=pltpu.VMEM)] * 7,
        out_specs=pl.BlockSpec(memory_space=pltpu.VMEM),
        scratch_shapes=[
            pltpu.VMEM((ROWS, 3, frame, width), jnp.bfloat16),
            pltpu.VMEM((ROWS, frame, width), jnp.bfloat16),
        ],
        compiler_params=pltpu.CompilerParams(vmem_limit_bytes=40 * 1024 * 1024),
        name="network",
    )(tiles, first, inner, last, row_mask(groups + 4, 2), row_mask(groups + 2, 1), inside)
    result = result.reshape(groups, ROWS, channels, cols)
    return jnp.transpose(result, (2, 0, 1, 3)).reshape(channels, rows, cols)


def rotation(rows_len, cols_len, modulus, direction):
    first_index = jnp.arange(rows_len, dtype=jnp.int32)
    second_index = jnp.arange(cols_len, dtype=jnp.int32)
    phase_index = first_index[:, None] * second_index[None, :] % modulus
    angles = phase_index.astype(jnp.float32) * (direction * 2.0 * math.pi / modulus)
    return (jnp.cos(angles), jnp.sin(angles))


def complex_dot(matrix_pair, data_pair, contracting):
    product = partial(
        lax.dot_general,
        dimension_numbers=(contracting, ((), ())),
        precision=lax.Precision.HIGH,
        preferred_element_type=jnp.float32,
    )
    return (
        product(matrix_pair[0], data_pair[0]) - product(matrix_pair[1], data_pair[1]),
        product(matrix_pair[0], data_pair[1]) + product(matrix_pair[1], data_pair[0]),
    )


def complex_mul(first_pair, second_pair):
    return (
        first_pair[0] * second_pair[0] - first_pair[1] * second_pair[1],
        first_pair[0] * second_pair[1] + first_pair[1] * second_pair[0],
    )


def transform_last(data_pair, outer_len, direction):
    vectors, length = data_pair[0].shape
    inner_len = length // outer_len
    shaped = (
        data_pair[0].reshape(vectors, outer_len, inner_len),
        data_pair[1].reshape(vectors, outer_len, inner_len),
    )
    sectioned = complex_dot(
        rotation(outer_len, outer_len, outer_len, direction), shaped, ((1,), (1,))
    )
    twiddles = rotation(outer_len, inner_len, length, direction)
    twisted = complex_mul(sectioned, (twiddles[0][:, None, :], twiddles[1][:, None, :]))
    finished = complex_dot(
        rotation(inner_len, inner_len, inner_len, direction), twisted, ((1,), (2,))
    )
    factor = 1.0 / math.sqrt(length)
    return (
        finished[0].reshape(length, vectors) * factor,
        finished[1].reshape(length, vectors) * factor,
    )


def transform_first(data_pair, outer_len, direction):
    length, vectors = data_pair[0].shape
    inner_len = length // outer_len
    shaped = (
        data_pair[0].reshape(outer_len, inner_len, vectors),
        data_pair[1].reshape(outer_len, inner_len, vectors),
    )
    sectioned = complex_dot(
        rotation(outer_len, outer_len, outer_len, direction), shaped, ((1,), (0,))
    )
    twiddles = rotation(outer_len, inner_len, length, direction)
    twisted = complex_mul(sectioned, (twiddles[0][:, :, None], twiddles[1][:, :, None]))
    finished = complex_dot(
        rotation(inner_len, inner_len, inner_len, direction), twisted, ((1,), (1,))
    )
    factor = 1.0 / math.sqrt(length)
    return (
        finished[0].reshape(length, vectors) * factor,
        finished[1].reshape(length, vectors) * factor,
    )


def split_pair(real, imag, axis):
    both = jnp.concatenate([real, imag], axis=axis)
    high = both.astype(jnp.bfloat16)
    low = (both - high.astype(jnp.float32)).astype(jnp.bfloat16)
    return jnp.concatenate([high, low, high], axis=axis)


def pair_matrix(inner, length, transposed):
    angles = np.outer(np.arange(inner), np.arange(inner)) % inner * (2.0 * np.pi / inner)
    cosines, sines = np.cos(angles), np.sin(angles)
    matrix = np.block([[cosines, sines], [-sines, cosines]]) / np.sqrt(length)
    if transposed:
        matrix = matrix.T
    high = matrix.astype(jnp.bfloat16)
    low = (matrix - high.astype(np.float64)).astype(jnp.bfloat16)
    return high, low


def twiddle_rows(outer, inner):
    angles = np.outer(np.arange(outer), np.arange(inner)) * (2.0 * np.pi / (outer * inner))
    return np.stack([np.cos(angles), np.sin(angles)], axis=1).astype(np.float32)


def turn(pair, twiddle_ref, index, sign):
    if index == 0:
        return pair
    cosine = twiddle_ref[index, 0:1]
    sine = sign * twiddle_ref[index, 1:2]
    return (pair[0] * cosine - pair[1] * sine, pair[0] * sine + pair[1] * cosine)


def pack(stage_ref, sent_ref, chunk):
    groups, body, _ = stage_ref.shape
    planes = body // PIECE
    tail = sent_ref.shape[2] - body

    def step(g, carry):
        powers = []
        for plane in range(planes):
            spot = slice(plane * PIECE, (plane + 1) * PIECE)
            values = stage_ref[g, spot, :]
            top = jnp.maximum(jnp.max(jnp.abs(values), axis=0, keepdims=True), 1e-30)
            power = jnp.ceil(jnp.log2(top)) - 14.0
            coded = jnp.round(values * jnp.exp2(-power))
            sent_ref[chunk, g, spot, :] = coded.astype(jnp.int32).astype(jnp.int16)
            powers.append(power)
        powers.append(jnp.zeros((tail - planes, power.shape[1]), jnp.float32))
        powers = jnp.concatenate(powers, axis=0)
        sent_ref[chunk, g, body:, :] = powers.astype(jnp.int32).astype(jnp.int16)
        return carry

    lax.fori_loop(0, groups, step, 0)


def unpack(got_ref, chunk, g, first, count, body):
    powers = got_ref[chunk, g, body:, :].astype(jnp.int32).astype(jnp.float32)
    scales = jnp.exp2(powers)
    pieces = []
    for plane in range(first, first + count):
        values = got_ref[chunk, g, plane * PIECE : (plane + 1) * PIECE, :]
        values = values.astype(jnp.int32).astype(jnp.float32)
        pieces.append(values * scales[plane : plane + 1])
    return pieces


def columns_part(chunk, clean_ref, maps_ref, matrix_ref, twiddle_ref, stage_ref):
    rows, full = maps_ref.shape[2:]
    groups = stage_ref.shape[0]
    inner = full // 3
    root = math.sqrt(0.75)
    clean = (clean_ref[0], clean_ref[1])
    image = [
        complex_mul((maps_ref[coil, 0], maps_ref[coil, 1]), clean)
        for coil in (2 * chunk, 2 * chunk + 1)
    ]
    image = [jnp.concatenate([image[0][part], image[1][part]], axis=0) for part in range(2)]
    first, second, third = [
        (image[0][:, n * inner : (n + 1) * inner], image[1][:, n * inner : (n + 1) * inner])
        for n in range(3)
    ]
    total = (second[0] + third[0], second[1] + third[1])
    apart = (root * (second[0] - third[0]), root * (second[1] - third[1]))
    middle = (first[0] - 0.5 * total[0], first[1] - 0.5 * total[1])
    bins = (
        (first[0] + total[0], first[1] + total[1]),
        (middle[0] + apart[1], middle[1] - apart[0]),
        (middle[0] - apart[1], middle[1] + apart[0]),
    )
    for index in range(3):
        turned = turn(bins[index], twiddle_ref, index, -1.0)
        result = lax.dot_general(
            matrix_ref[...],
            split_pair(turned[0], turned[1], 1),
            (((1,), (1,)), ((), ())),
            preferred_element_type=jnp.float32,
        )
        for part in range(2):
            for which in range(2):
                base = ((part * 2 + which) * 3 + index) * PIECE
                block = result[part * inner : (part + 1) * inner]
                block = block[:, which * rows : (which + 1) * rows]
                stage_ref[:, base : base + PIECE, :] = block.reshape(groups, PIECE, rows)


def rows_part(
    chunk, got_ref, targets_ref, keep_ref, permute_ref, forward_ref, inverse_ref, twiddle_ref, stage_ref
):
    groups, body, rows = stage_ref.shape
    vectors = body // 2
    planes = vectors // PIECE
    height = groups * rows
    inner = height // 4
    copies = vectors // keep_ref.shape[0]
    whole = [
        jnp.concatenate(
            [
                jnp.concatenate(unpack(got_ref, chunk, g, part * planes, planes, body), axis=0)
                for g in range(groups)
            ],
            axis=1,
        )
        for part in range(2)
    ]
    a0, a1, a2, a3 = [
        (whole[0][:, n * inner : (n + 1) * inner], whole[1][:, n * inner : (n + 1) * inner])
        for n in range(4)
    ]
    even = (a0[0] + a2[0], a0[1] + a2[1])
    odd = (a0[0] - a2[0], a0[1] - a2[1])
    even_next = (a1[0] + a3[0], a1[1] + a3[1])
    odd_next = (a1[0] - a3[0], a1[1] - a3[1])
    bins = (
        (even[0] + even_next[0], even[1] + even_next[1]),
        (odd[0] + odd_next[1], odd[1] - odd_next[0]),
        (even[0] - even_next[0], even[1] - even_next[1]),
        (odd[0] - odd_next[1], odd[1] + odd_next[0]),
    )
    turned_back = []
    for index in range(4):
        turned = turn(bins[index], twiddle_ref, index, -1.0)
        spectrum = jnp.dot(
            split_pair(turned[0], turned[1], 1),
            forward_ref[...],
            preferred_element_type=jnp.float32,
        )
        lanes = slice(index * inner, (index + 1) * inner)
        keep = jnp.concatenate([keep_ref[:, lanes]] * copies, axis=0)
        spots = slice(chunk * vectors, (chunk + 1) * vectors)
        residual = [
            keep
            * (spectrum[:, part * inner : (part + 1) * inner] - targets_ref[part, spots, lanes])
            for part in range(2)
        ]
        inverse = jnp.dot(
            split_pair(residual[0], residual[1], 1),
            inverse_ref[...],
            preferred_element_type=jnp.float32,
        )
        turned_back.append(turn((inverse[:, :inner], inverse[:, inner:]), twiddle_ref, index, 1.0))
    c0, c1, c2, c3 = turned_back
    even = (c0[0] + c2[0], c0[1] + c2[1])
    odd = (c0[0] - c2[0], c0[1] - c2[1])
    even_next = (c1[0] + c3[0], c1[1] + c3[1])
    odd_next = (c1[0] - c3[0], c1[1] - c3[1])
    blocks = (
        (even[0] + even_next[0], even[1] + even_next[1]),
        (odd[0] - odd_next[1], odd[1] + odd_next[0]),
        (even[0] - even_next[0], even[1] - even_next[1]),
        (odd[0] + odd_next[1], odd[1] - odd_next[0]),
    )
    per_block = inner // rows
    for g in range(groups):
        lanes = slice((g % per_block) * rows, (g % per_block + 1) * rows)
        for part in range(2):
            stage_ref[g, part * vectors : (part + 1) * vectors, :] = blocks[g // per_block][part][
                :, lanes
            ]


def combine_part(chunk, got_ref, maps_ref, matrix_ref, twiddle_ref, body, out_ref):
    rows, full = maps_ref.shape[2:]
    groups = got_ref.shape[1]
    inner = full // 3
    root = math.sqrt(0.75)

    def plane(part, coil, index):
        spot = (part * 2 + coil) * 3 + index
        return jnp.concatenate(
            [unpack(got_ref, chunk, g, spot, 1, body)[0] for g in range(groups)], axis=0
        )

    turned = []
    for index in range(3):
        parts = [
            jnp.concatenate([plane(part, coil, index) for coil in range(2)], axis=1)
            for part in range(2)
        ]
        result = lax.dot_general(
            split_pair(parts[0], parts[1], 0),
            matrix_ref[...],
            (((0,), (0,)), ((), ())),
            preferred_element_type=jnp.float32,
        )
        turned.append(turn((result[:, :inner], result[:, inner:]), twiddle_ref, index, 1.0))
    c0, c1, c2 = turned
    total = (c1[0] + c2[0], c1[1] + c2[1])
    apart = (root * (c1[0] - c2[0]), root * (c1[1] - c2[1]))
    middle = (c0[0] - 0.5 * total[0], c0[1] - 0.5 * total[1])
    blocks = (
        (c0[0] + total[0], c0[1] + total[1]),
        (middle[0] - apart[1], middle[1] + apart[0]),
        (middle[0] + apart[1], middle[1] - apart[0]),
    )
    share = out_ref.shape[3]
    for start in range(0, full, 128):
        n, inside = start // inner, slice(start % inner, start % inner + 128)
        lanes = slice(start, start + 128)
        half, place = start // share, slice(start % share, start % share + 128)
        real = 0.0 if chunk == 0 else out_ref[half, 0, :, place]
        imag = 0.0 if chunk == 0 else out_ref[half, 1, :, place]
        for coil in range(2):
            back = [
                blocks[n][part][coil * rows : (coil + 1) * rows, inside] for part in range(2)
            ]
            map_real = maps_ref[2 * chunk + coil, 0, :, lanes]
            map_imag = maps_ref[2 * chunk + coil, 1, :, lanes]
            real = real + map_real * back[0] + map_imag * back[1]
            imag = imag + map_real * back[1] - map_imag * back[0]
        out_ref[half, 0, :, place] = real
        out_ref[half, 1, :, place] = imag


def consistency_kernel(
    clean_ref,
    maps_ref,
    left_ref,
    columns_twiddle_ref,
    rows_twiddle_ref,
    sampled_ref,
    targets_hbm,
    permute_hbm,
    forward_hbm,
    inverse_hbm,
    right_hbm,
    out_ref,
    targets_ref,
    permute_ref,
    forward_ref,
    inverse_ref,
    right_ref,
    keep_ref,
    stage_ref,
    sent_first,
    got_first,
    sent_second,
    got_second,
    load_sem,
    send_sem,
    recv_sem,
):
    groups, body, _ = stage_ref.shape
    chunks = sent_first.shape[0]
    me = lax.axis_index("gz")
    buffers = ((sent_first, got_first), (sent_second, got_second))

    def peer_of(k):
        return lax.rem(me + k, groups)

    def copy(trip, chunk, target, slot):
        sent, got = buffers[trip]
        return pltpu.make_async_remote_copy(
            src_ref=sent.at[chunk, target],
            dst_ref=got.at[chunk, slot],
            send_sem=send_sem.at[trip, chunk, target],
            recv_sem=recv_sem.at[trip, chunk, slot],
            device_id={"gz": target},
            device_id_type=pl.DeviceIdType.MESH,
        )

    def over_peers(action):
        def step(k, carry):
            action(peer_of(k))
            return carry

        lax.fori_loop(1, groups, step, 0)

    def send(trip, chunk):
        sent, got = buffers[trip]
        over_peers(lambda peer: copy(trip, chunk, peer, me).start())
        got[chunk, me] = sent[chunk, me]

    def receive(trip, chunk):
        over_peers(lambda peer: copy(trip, chunk, peer, peer).wait_recv())

    barrier = pltpu.get_barrier_semaphore()
    over_peers(
        lambda peer: pl.semaphore_signal(
            barrier, inc=1, device_id={"gz": peer}, device_id_type=pl.DeviceIdType.MESH
        )
    )
    loads = [
        pltpu.make_async_copy(source, target, load_sem.at[i])
        for i, (source, target) in enumerate(
            (
                (targets_hbm, targets_ref),
                (permute_hbm, permute_ref),
                (forward_hbm, forward_ref),
                (inverse_hbm, inverse_ref),
                (right_hbm, right_ref),
            )
        )
    ]
    for load in loads:
        load.start()
    for chunk in range(chunks):
        columns_part(chunk, clean_ref, maps_ref, left_ref, columns_twiddle_ref, stage_ref)
        pack(stage_ref, sent_first, chunk)
        if chunk == 0:
            pl.semaphore_wait(barrier, groups - 1)
        send(0, chunk)
    for load in loads:
        load.wait()
    keep_ref[...] = jnp.dot(
        sampled_ref[...], permute_ref[...], preferred_element_type=jnp.float32
    )
    for part in range(2):
        values = targets_ref[part]
        high = values.astype(jnp.bfloat16)
        low = (values - high.astype(jnp.float32)).astype(jnp.bfloat16)
        targets_ref[part] = jnp.dot(
            high, permute_ref[...], preferred_element_type=jnp.float32
        ) + jnp.dot(low, permute_ref[...], preferred_element_type=jnp.float32)
    for chunk in range(chunks):
        receive(0, chunk)
        rows_part(
            chunk,
            got_first,
            targets_ref,
            keep_ref,
            permute_ref,
            forward_ref,
            inverse_ref,
            rows_twiddle_ref,
            stage_ref,
        )
        pack(stage_ref, sent_second, chunk)
        send(1, chunk)
    for chunk in range(chunks):
        receive(1, chunk)
        combine_part(
            chunk, got_second, maps_ref, right_ref, columns_twiddle_ref, body, out_ref
        )
    for trip in range(2):
        for chunk in range(chunks):
            over_peers(lambda peer: copy(trip, chunk, peer, me).wait_send())


def aligned_gradient(clean_wide, coil_maps, measured, sampled):
    coils, _, rows, full = coil_maps.shape
    groups = lax.axis_size("gz")
    height = rows * groups
    inner = full // 3
    chunks = coils // 2
    body = 2 * 2 * 3 * PIECE
    halves = lax.axis_size("col")
    high, low = pair_matrix(inner, full, False)
    left = np.concatenate([high, high, low], axis=1)
    right = np.concatenate([high, high, low], axis=0)
    rows_high, rows_low = pair_matrix(height // 4, height, True)
    back_high, back_low = pair_matrix(height // 4, height, False)
    forward = np.concatenate([rows_high, rows_high, rows_low], axis=0)
    inverse = np.concatenate([back_high, back_high, back_low], axis=0)
    place = np.arange(height)
    source = place // (height // 4) + 4 * (place % (height // 4))
    permute = (place[:, None] == source[None, :]).astype(jnp.bfloat16)
    targets = jnp.transpose(measured.reshape(2, PIECE, 3, coils, height), (0, 3, 2, 1, 4))
    targets = targets.reshape(2, coils * 3 * PIECE, height)
    keep = jnp.transpose(sampled.reshape(PIECE, 3, height), (1, 0, 2)).astype(jnp.bfloat16)
    keep = keep.reshape(3 * PIECE, height)
    vmem, anywhere = pl.BlockSpec(memory_space=pltpu.VMEM), pl.BlockSpec(memory_space=pl.ANY)
    wire = pltpu.VMEM((chunks, groups, body + 16, rows), jnp.int16)
    return pl.pallas_call(
        consistency_kernel,
        out_shape=jax.ShapeDtypeStruct((halves, 2, rows, full // halves), jnp.float32),
        in_specs=[vmem] * 6 + [anywhere] * 5,
        out_specs=vmem,
        scratch_shapes=[
            pltpu.VMEM(targets.shape, jnp.float32),
            pltpu.VMEM(permute.shape, jnp.bfloat16),
            pltpu.VMEM(forward.shape, jnp.bfloat16),
            pltpu.VMEM(inverse.shape, jnp.bfloat16),
            pltpu.VMEM(right.shape, jnp.bfloat16),
            pltpu.VMEM(keep.shape, jnp.float32),
            pltpu.VMEM((groups, body, rows), jnp.float32),
            wire,
            wire,
            wire,
            wire,
            pltpu.SemaphoreType.DMA((5,)),
            pltpu.SemaphoreType.DMA((2, chunks, groups)),
            pltpu.SemaphoreType.DMA((2, chunks, groups)),
        ],
        compiler_params=pltpu.CompilerParams(
            vmem_limit_bytes=56 * 1024 * 1024, collective_id=0, has_side_effects=True
        ),
        name="consistency",
    )(
        clean_wide,
        coil_maps,
        left,
        twiddle_rows(3, inner),
        twiddle_rows(4, height // 4),
        keep,
        targets,
        permute,
        forward,
        inverse,
        right,
    )


def gradient(clean_wide, coil_maps, measured, sampled):
    coils, _, rows, full = coil_maps.shape
    groups = lax.axis_size("gz")
    whole = rows == 128 and coils % 2 == 0 and full == 3 * PIECE * groups
    if whole and (rows * groups) % 1024 == 0 and full % 768 == 0:
        return aligned_gradient(clean_wide, coil_maps, measured, sampled)
    grad = plain_gradient(clean_wide, coil_maps, measured, sampled)
    return jnp.stack(jnp.split(grad, lax.axis_size("col"), axis=2))


def plain_gradient(clean_wide, coil_maps, measured, sampled):
    maps_real = coil_maps[:, 0]
    maps_imag = coil_maps[:, 1]
    coil_count, row_count, full_cols = maps_real.shape
    coil_pair = complex_mul((maps_real, maps_imag), (clean_wide[0][None], clean_wide[1][None]))
    spectra = transform_last(
        (
            coil_pair[0].reshape(coil_count * row_count, full_cols),
            coil_pair[1].reshape(coil_count * row_count, full_cols),
        ),
        W_FAC,
        -1.0,
    )
    groups = lax.axis_size("gz")
    pencil = full_cols // groups
    arrived = (
        lax.all_to_all(
            spectra[0].reshape(groups, pencil, coil_count, row_count),
            "gz",
            split_axis=0,
            concat_axis=3,
            tiled=True,
        ),
        lax.all_to_all(
            spectra[1].reshape(groups, pencil, coil_count, row_count),
            "gz",
            split_axis=0,
            concat_axis=3,
            tiled=True,
        ),
    )
    item_count = arrived[0].shape[2]
    height = arrived[0].shape[3]
    flattened = (
        arrived[0].reshape(pencil * item_count, height),
        arrived[1].reshape(pencil * item_count, height),
    )
    transformed = transform_last(flattened, H_FAC, -1.0)
    keeping = sampled.astype(jnp.float32)[:, None, :]
    resid_real = keeping * (transformed[0].T.reshape(pencil, item_count, height) - measured[0])
    resid_imag = keeping * (transformed[1].T.reshape(pencil, item_count, height) - measured[1])
    height = resid_real.shape[2]
    inverse = transform_last(
        (
            resid_real.reshape(pencil * coil_count, height),
            resid_imag.reshape(pencil * coil_count, height),
        ),
        H_FAC,
        1.0,
    )
    arrived = (
        lax.all_to_all(
            inverse[0].T.reshape(pencil, coil_count, groups, row_count),
            "gz",
            split_axis=2,
            concat_axis=0,
            tiled=True,
        ),
        lax.all_to_all(
            inverse[1].T.reshape(pencil, coil_count, groups, row_count),
            "gz",
            split_axis=2,
            concat_axis=0,
            tiled=True,
        ),
    )
    item_count = arrived[0].shape[1]
    flattened = (
        arrived[0].reshape(full_cols, item_count * row_count),
        arrived[1].reshape(full_cols, item_count * row_count),
    )
    transformed = transform_first(flattened, W_FAC, 1.0)
    back_real = jnp.transpose(transformed[0].reshape(full_cols, item_count, row_count), (1, 2, 0))
    back_imag = jnp.transpose(transformed[1].reshape(full_cols, item_count, row_count), (1, 2, 0))
    grad_real = jnp.sum(maps_real * back_real + maps_imag * back_imag, axis=0)
    grad_imag = jnp.sum(maps_real * back_imag - maps_imag * back_real, axis=0)
    return jnp.stack([grad_real, grad_imag])


def local(
    noisy_image, fresh_noise, coil_maps, measured, sampled, first_kernel, inner_kernels, last_kernel
):
    predicted = network(noisy_image, first_kernel, inner_kernels, last_kernel)
    clean = (noisy_image - SIGMA_NOW * predicted) / SCALE_NOW
    clean_wide = lax.all_gather(clean, "col", axis=2, tiled=True)
    grad = gradient(clean_wide, coil_maps, measured, sampled)
    if lax.axis_size("col") == 2:
        here = lax.axis_index("col")
        away = lax.dynamic_index_in_dim(grad, 1 - here, 0, keepdims=False)
        grad_tile = lax.dynamic_index_in_dim(grad, here, 0, keepdims=False)
        grad_tile = grad_tile + lax.ppermute(away, "col", [(0, 1), (1, 0)])
    else:
        grad_tile = lax.psum_scatter(grad, "col", scatter_dimension=0, tiled=False)
    update = clean - STEP_GAIN * grad_tile
    return SCALE_NEXT * update + DIRECT_GAIN * predicted + NOISE_GAIN * fresh_noise


def solution(mesh):
    in_specs = (
        P("grp", "gz", "col"),
        P("grp", "gz", "col"),
        P("col", "grp", "gz", None),
        P("grp", "gz", "col", None),
        P("gz", "grp"),
        P(),
        P(),
        P(),
    )
    out_specs = P("grp", "gz", "col")
    return jax.shard_map(local, mesh=mesh, in_specs=in_specs, out_specs=out_specs, check_vma=False)
```

```python
from functools import partial
import math

import jax
import jax.numpy as jnp
import numpy as np
from jax import lax
from jax.experimental import pallas as pl
from jax.experimental.pallas import tpu as pltpu
from jax.sharding import PartitionSpec as P

H_FAC = 8
W_FAC = 6
ROWS = 4
PIECE = 32


SCALE_NOW = 0.8
SIGMA_NOW = 0.6
STEP_GAIN = 1.0
SCALE_NEXT = 0.9
DIRECT_GAIN = 0.31622776601683794
NOISE_GAIN = 0.3


def with_halo(block, sides, width):
    for axis, dim in sides:
        count = lax.axis_size(axis)
        forward = [(i, i + 1) for i in range(count - 1)]
        backward = [(target, source) for source, target in forward]
        low = lax.ppermute(
            lax.slice_in_dim(block, block.shape[dim] - width, None, axis=dim), axis, forward
        )
        high = lax.ppermute(lax.slice_in_dim(block, 0, width, axis=dim), axis, backward)
        block = jnp.concatenate([low, block, high], axis=dim)
    return block


def row_banded(kernel, span):
    taps = kernel.reshape(3, 3, kernel.shape[1], kernel.shape[2])
    return jnp.stack(
        [
            jnp.pad(taps, ((start, span - 3 - start), (0, 0), (0, 0), (0, 0)))
            for start in range(span - 2)
        ]
    )


def network_kernel(
    groups,
    cols,
    tiles_ref,
    first_ref,
    inner_ref,
    last_ref,
    first_rows_ref,
    inner_rows_ref,
    inside_ref,
    out_ref,
    first_held,
    inner_held,
):
    frame, width = inside_ref.shape
    half = width // 2

    def act(halved, keep):
        return (halved + halved * jnp.tanh(halved)) * (inside_ref[...] * keep)

    def first_layer(group):
        halved = jnp.dot(
            tiles_ref[group // ROWS],
            first_ref[lax.rem(group, ROWS)],
            preferred_element_type=jnp.float32,
        )
        hidden = act(halved, first_rows_ref[group])
        slot = lax.rem(group, ROWS)
        first_held[slot, 0] = pltpu.roll(hidden, 1, 0).astype(jnp.bfloat16)
        first_held[slot, 1] = hidden.astype(jnp.bfloat16)
        first_held[slot, 2] = pltpu.roll(hidden, frame - 1, 0).astype(jnp.bfloat16)

    def inner_layer(group):
        slot = lax.rem(group, ROWS)
        after = lax.rem(group + 1, ROWS)
        total = None
        for shift in range(3):
            part = jnp.dot(
                first_held[slot, shift],
                inner_ref[shift, :width],
                preferred_element_type=jnp.float32,
            ) + jnp.dot(
                first_held[after, shift, :, :half],
                inner_ref[shift, width:],
                preferred_element_type=jnp.float32,
            )
            total = part if total is None else total + part
        inner_held[slot] = act(total, inner_rows_ref[group]).astype(jnp.bfloat16)

    def last_layer(group):
        slot = lax.rem(group, ROWS)
        after = lax.rem(group + 1, ROWS)
        lanes = (((1,), (1,)), ((), ()))
        part = lax.dot_general(
            last_ref[:, :width], inner_held[slot], lanes, preferred_element_type=jnp.float32
        ) + lax.dot_general(
            last_ref[:, width:],
            inner_held[after, :, :half],
            lanes,
            preferred_element_type=jnp.float32,
        )
        left = part[:8]
        left = jnp.concatenate([left[:, frame - 1 :], left[:, : cols - 1]], axis=1)
        out_ref[group] = left + part[8:16, :cols] + part[16:24, 1 : cols + 1]

    for group in range(4):
        first_layer(group)
    for group in range(2):
        inner_layer(group)

    def step(group, carry):
        last_layer(group)
        inner_layer(group + 2)
        first_layer(group + 4)
        return carry

    lax.fori_loop(0, groups, step, 0)


def network(image, first_kernel, inner_kernels, last_kernel):
    channels, rows, cols = image.shape
    hidden = first_kernel.shape[1]
    groups = rows // ROWS
    frame = cols + 16
    width = ROWS * hidden
    span = ROWS * ROWS + 2
    tile_count = groups // ROWS + 1
    padded = with_halo(image.astype(jnp.bfloat16), (("gz", 1), ("col", 2)), 3)
    padded = jnp.pad(padded, ((0, 0), (0, ROWS * ROWS * tile_count + 2 - rows - 6), (0, 0)))
    gap = jnp.zeros(padded.shape[:2] + (frame - cols - 6,), padded.dtype)
    ring = jnp.concatenate([padded[:, :, 3:], gap, padded[:, :, :3]], axis=2)
    shifted = jnp.stack([jnp.roll(ring, 1 - shift, axis=2) for shift in range(3)])
    tiles = jnp.stack(
        [shifted[:, :, ROWS * ROWS * t : ROWS * ROWS * t + span] for t in range(tile_count)]
    )
    depth = 3 * channels * span
    tiles = jnp.transpose(tiles.reshape(tile_count, depth, frame), (0, 2, 1))
    tiles = jnp.pad(tiles, ((0, 0), (0, 0), (0, 128 - depth)))
    half = jnp.asarray(0.5, jnp.bfloat16)
    first = jnp.transpose(row_banded(first_kernel * half, span), (2, 4, 1, 0, 3))
    first = first.reshape(depth, ROWS, width)
    first = jnp.pad(jnp.transpose(first, (1, 0, 2)), ((0, 0), (0, 128 - depth), (0, 0)))
    inner = jnp.transpose(row_banded(inner_kernels[0] * half, ROWS + 2), (2, 1, 4, 0, 3))
    inner = inner.reshape(3, (ROWS + 2) * hidden, width)
    last = jnp.transpose(row_banded(last_kernel, ROWS + 2), (2, 0, 3, 1, 4))
    last = last.reshape(3 * ROWS * channels, (ROWS + 2) * hidden)
    last = jnp.pad(last, ((0, 32 - last.shape[0]), (0, 0)))
    top = lax.axis_index("gz") * rows
    height = rows * lax.axis_size("gz")
    across = cols * lax.axis_size("col")

    def row_mask(count, offset):
        place = top + ROWS * jnp.arange(count)[:, None] + jnp.arange(ROWS)[None, :] - offset
        keep = ((place >= 0) & (place < height)).astype(jnp.float32)
        return jnp.repeat(keep, hidden, axis=1).reshape(count, 1, width)

    spot = jnp.arange(frame)
    spot = jnp.where(spot < cols + 8, spot, spot - frame) + lax.axis_index("col") * cols
    inside = ((spot >= 0) & (spot < across)).astype(jnp.float32)
    inside = jnp.broadcast_to(inside[:, None], (frame, width))
    result = pl.pallas_call(
        partial(network_kernel, groups, cols),
        out_shape=jax.ShapeDtypeStruct((groups, ROWS * channels, cols), jnp.float32),
        in_specs=[pl.BlockSpec(memory_space=pltpu.VMEM)] * 7,
        out_specs=pl.BlockSpec(memory_space=pltpu.VMEM),
        scratch_shapes=[
            pltpu.VMEM((ROWS, 3, frame, width), jnp.bfloat16),
            pltpu.VMEM((ROWS, frame, width), jnp.bfloat16),
        ],
        compiler_params=pltpu.CompilerParams(vmem_limit_bytes=40 * 1024 * 1024),
        name="network",
    )(tiles, first, inner, last, row_mask(groups + 4, 2), row_mask(groups + 2, 1), inside)
    result = result.reshape(groups, ROWS, channels, cols)
    return jnp.transpose(result, (2, 0, 1, 3)).reshape(channels, rows, cols)


def rotation(rows_len, cols_len, modulus, direction):
    first_index = jnp.arange(rows_len, dtype=jnp.int32)
    second_index = jnp.arange(cols_len, dtype=jnp.int32)
    phase_index = first_index[:, None] * second_index[None, :] % modulus
    angles = phase_index.astype(jnp.float32) * (direction * 2.0 * math.pi / modulus)
    return (jnp.cos(angles), jnp.sin(angles))


def complex_dot(matrix_pair, data_pair, contracting):
    product = partial(
        lax.dot_general,
        dimension_numbers=(contracting, ((), ())),
        precision=lax.Precision.HIGH,
        preferred_element_type=jnp.float32,
    )
    return (
        product(matrix_pair[0], data_pair[0]) - product(matrix_pair[1], data_pair[1]),
        product(matrix_pair[0], data_pair[1]) + product(matrix_pair[1], data_pair[0]),
    )


def complex_mul(first_pair, second_pair):
    return (
        first_pair[0] * second_pair[0] - first_pair[1] * second_pair[1],
        first_pair[0] * second_pair[1] + first_pair[1] * second_pair[0],
    )


def transform_last(data_pair, outer_len, direction):
    vectors, length = data_pair[0].shape
    inner_len = length // outer_len
    shaped = (
        data_pair[0].reshape(vectors, outer_len, inner_len),
        data_pair[1].reshape(vectors, outer_len, inner_len),
    )
    sectioned = complex_dot(
        rotation(outer_len, outer_len, outer_len, direction), shaped, ((1,), (1,))
    )
    twiddles = rotation(outer_len, inner_len, length, direction)
    twisted = complex_mul(sectioned, (twiddles[0][:, None, :], twiddles[1][:, None, :]))
    finished = complex_dot(
        rotation(inner_len, inner_len, inner_len, direction), twisted, ((1,), (2,))
    )
    factor = 1.0 / math.sqrt(length)
    return (
        finished[0].reshape(length, vectors) * factor,
        finished[1].reshape(length, vectors) * factor,
    )


def transform_first(data_pair, outer_len, direction):
    length, vectors = data_pair[0].shape
    inner_len = length // outer_len
    shaped = (
        data_pair[0].reshape(outer_len, inner_len, vectors),
        data_pair[1].reshape(outer_len, inner_len, vectors),
    )
    sectioned = complex_dot(
        rotation(outer_len, outer_len, outer_len, direction), shaped, ((1,), (0,))
    )
    twiddles = rotation(outer_len, inner_len, length, direction)
    twisted = complex_mul(sectioned, (twiddles[0][:, :, None], twiddles[1][:, :, None]))
    finished = complex_dot(
        rotation(inner_len, inner_len, inner_len, direction), twisted, ((1,), (1,))
    )
    factor = 1.0 / math.sqrt(length)
    return (
        finished[0].reshape(length, vectors) * factor,
        finished[1].reshape(length, vectors) * factor,
    )


def split_pair(real, imag, axis):
    both = jnp.concatenate([real, imag], axis=axis)
    high = both.astype(jnp.bfloat16)
    low = (both - high.astype(jnp.float32)).astype(jnp.bfloat16)
    return jnp.concatenate([high, low, high], axis=axis)


def pair_matrix(inner, length, transposed):
    angles = np.outer(np.arange(inner), np.arange(inner)) % inner * (2.0 * np.pi / inner)
    cosines, sines = np.cos(angles), np.sin(angles)
    matrix = np.block([[cosines, sines], [-sines, cosines]]) / np.sqrt(length)
    if transposed:
        matrix = matrix.T
    high = matrix.astype(jnp.bfloat16)
    low = (matrix - high.astype(np.float64)).astype(jnp.bfloat16)
    return high, low


def twiddle_rows(outer, inner):
    angles = np.outer(np.arange(outer), np.arange(inner)) * (2.0 * np.pi / (outer * inner))
    return np.stack([np.cos(angles), np.sin(angles)], axis=1).astype(np.float32)


def turn(pair, twiddle_ref, index, sign):
    if index == 0:
        return pair
    cosine = twiddle_ref[index, 0:1]
    sine = sign * twiddle_ref[index, 1:2]
    return (pair[0] * cosine - pair[1] * sine, pair[0] * sine + pair[1] * cosine)


def pack(stage_ref, sent_ref, chunk):
    groups, body, _ = stage_ref.shape
    planes = body // PIECE
    tail = sent_ref.shape[2] - body

    def step(g, carry):
        powers = []
        for plane in range(planes):
            spot = slice(plane * PIECE, (plane + 1) * PIECE)
            values = stage_ref[g, spot, :]
            top = jnp.maximum(jnp.max(jnp.abs(values), axis=0, keepdims=True), 1e-30)
            power = jnp.ceil(jnp.log2(top)) - 14.0
            coded = jnp.round(values * jnp.exp2(-power))
            sent_ref[chunk, g, spot, :] = coded.astype(jnp.int32).astype(jnp.int16)
            powers.append(power)
        powers.append(jnp.zeros((tail - planes, power.shape[1]), jnp.float32))
        powers = jnp.concatenate(powers, axis=0)
        sent_ref[chunk, g, body:, :] = powers.astype(jnp.int32).astype(jnp.int16)
        return carry

    lax.fori_loop(0, groups, step, 0)


def unpack(got_ref, chunk, g, first, count, body):
    powers = got_ref[chunk, g, body:, :].astype(jnp.int32).astype(jnp.float32)
    scales = jnp.exp2(powers)
    pieces = []
    for plane in range(first, first + count):
        values = got_ref[chunk, g, plane * PIECE : (plane + 1) * PIECE, :]
        values = values.astype(jnp.int32).astype(jnp.float32)
        pieces.append(values * scales[plane : plane + 1])
    return pieces


def columns_part(chunk, clean_ref, maps_ref, matrix_ref, twiddle_ref, stage_ref):
    rows, full = maps_ref.shape[2:]
    groups = stage_ref.shape[0]
    inner = full // 3
    root = math.sqrt(0.75)
    clean = [
        jnp.concatenate([clean_ref[half, part] for half in range(clean_ref.shape[0])], axis=1)
        for part in range(2)
    ]
    image = [
        complex_mul((maps_ref[coil, 0], maps_ref[coil, 1]), clean)
        for coil in (2 * chunk, 2 * chunk + 1)
    ]
    image = [jnp.concatenate([image[0][part], image[1][part]], axis=0) for part in range(2)]
    first, second, third = [
        (image[0][:, n * inner : (n + 1) * inner], image[1][:, n * inner : (n + 1) * inner])
        for n in range(3)
    ]
    total = (second[0] + third[0], second[1] + third[1])
    apart = (root * (second[0] - third[0]), root * (second[1] - third[1]))
    middle = (first[0] - 0.5 * total[0], first[1] - 0.5 * total[1])
    bins = (
        (first[0] + total[0], first[1] + total[1]),
        (middle[0] + apart[1], middle[1] - apart[0]),
        (middle[0] - apart[1], middle[1] + apart[0]),
    )
    for index in range(3):
        turned = turn(bins[index], twiddle_ref, index, -1.0)
        result = lax.dot_general(
            matrix_ref[...],
            split_pair(turned[0], turned[1], 1),
            (((1,), (1,)), ((), ())),
            preferred_element_type=jnp.float32,
        )
        for part in range(2):
            for which in range(2):
                base = ((part * 2 + which) * 3 + index) * PIECE
                block = result[part * inner : (part + 1) * inner]
                block = block[:, which * rows : (which + 1) * rows]
                stage_ref[:, base : base + PIECE, :] = block.reshape(groups, PIECE, rows)


def rows_part(
    chunk, got_ref, targets_ref, keep_ref, permute_ref, forward_ref, inverse_ref, twiddle_ref, stage_ref
):
    groups, body, rows = stage_ref.shape
    vectors = body // 2
    planes = vectors // PIECE
    height = groups * rows
    inner = height // 4
    copies = vectors // keep_ref.shape[0]
    whole = [
        jnp.concatenate(
            [
                jnp.concatenate(unpack(got_ref, chunk, g, part * planes, planes, body), axis=0)
                for g in range(groups)
            ],
            axis=1,
        )
        for part in range(2)
    ]
    a0, a1, a2, a3 = [
        (whole[0][:, n * inner : (n + 1) * inner], whole[1][:, n * inner : (n + 1) * inner])
        for n in range(4)
    ]
    even = (a0[0] + a2[0], a0[1] + a2[1])
    odd = (a0[0] - a2[0], a0[1] - a2[1])
    even_next = (a1[0] + a3[0], a1[1] + a3[1])
    odd_next = (a1[0] - a3[0], a1[1] - a3[1])
    bins = (
        (even[0] + even_next[0], even[1] + even_next[1]),
        (odd[0] + odd_next[1], odd[1] - odd_next[0]),
        (even[0] - even_next[0], even[1] - even_next[1]),
        (odd[0] - odd_next[1], odd[1] + odd_next[0]),
    )
    turned_back = []
    for index in range(4):
        turned = turn(bins[index], twiddle_ref, index, -1.0)
        spectrum = jnp.dot(
            split_pair(turned[0], turned[1], 1),
            forward_ref[...],
            preferred_element_type=jnp.float32,
        )
        lanes = slice(index * inner, (index + 1) * inner)
        keep = jnp.concatenate([keep_ref[:, lanes]] * copies, axis=0)
        spots = slice(chunk * vectors, (chunk + 1) * vectors)
        residual = [
            keep
            * (spectrum[:, part * inner : (part + 1) * inner] - targets_ref[part, spots, lanes])
            for part in range(2)
        ]
        inverse = jnp.dot(
            split_pair(residual[0], residual[1], 1),
            inverse_ref[...],
            preferred_element_type=jnp.float32,
        )
        turned_back.append(turn((inverse[:, :inner], inverse[:, inner:]), twiddle_ref, index, 1.0))
    c0, c1, c2, c3 = turned_back
    even = (c0[0] + c2[0], c0[1] + c2[1])
    odd = (c0[0] - c2[0], c0[1] - c2[1])
    even_next = (c1[0] + c3[0], c1[1] + c3[1])
    odd_next = (c1[0] - c3[0], c1[1] - c3[1])
    blocks = (
        (even[0] + even_next[0], even[1] + even_next[1]),
        (odd[0] - odd_next[1], odd[1] + odd_next[0]),
        (even[0] - even_next[0], even[1] - even_next[1]),
        (odd[0] + odd_next[1], odd[1] - odd_next[0]),
    )
    per_block = inner // rows
    for g in range(groups):
        lanes = slice((g % per_block) * rows, (g % per_block + 1) * rows)
        for part in range(2):
            stage_ref[g, part * vectors : (part + 1) * vectors, :] = blocks[g // per_block][part][
                :, lanes
            ]


def combine_part(chunk, got_ref, maps_ref, matrix_ref, twiddle_ref, body, out_ref):
    rows, full = maps_ref.shape[2:]
    groups = got_ref.shape[1]
    inner = full // 3
    root = math.sqrt(0.75)

    def plane(part, coil, index):
        spot = (part * 2 + coil) * 3 + index
        return jnp.concatenate(
            [unpack(got_ref, chunk, g, spot, 1, body)[0] for g in range(groups)], axis=0
        )

    turned = []
    for index in range(3):
        parts = [
            jnp.concatenate([plane(part, coil, index) for coil in range(2)], axis=1)
            for part in range(2)
        ]
        result = lax.dot_general(
            split_pair(parts[0], parts[1], 0),
            matrix_ref[...],
            (((0,), (0,)), ((), ())),
            preferred_element_type=jnp.float32,
        )
        turned.append(turn((result[:, :inner], result[:, inner:]), twiddle_ref, index, 1.0))
    c0, c1, c2 = turned
    total = (c1[0] + c2[0], c1[1] + c2[1])
    apart = (root * (c1[0] - c2[0]), root * (c1[1] - c2[1]))
    middle = (c0[0] - 0.5 * total[0], c0[1] - 0.5 * total[1])
    blocks = (
        (c0[0] + total[0], c0[1] + total[1]),
        (middle[0] - apart[1], middle[1] + apart[0]),
        (middle[0] + apart[1], middle[1] - apart[0]),
    )
    share = out_ref.shape[3]
    for start in range(0, full, 128):
        n, inside = start // inner, slice(start % inner, start % inner + 128)
        lanes = slice(start, start + 128)
        half, place = start // share, slice(start % share, start % share + 128)
        real = 0.0 if chunk == 0 else out_ref[half, 0, :, place]
        imag = 0.0 if chunk == 0 else out_ref[half, 1, :, place]
        for coil in range(2):
            back = [
                blocks[n][part][coil * rows : (coil + 1) * rows, inside] for part in range(2)
            ]
            map_real = maps_ref[2 * chunk + coil, 0, :, lanes]
            map_imag = maps_ref[2 * chunk + coil, 1, :, lanes]
            real = real + map_real * back[0] + map_imag * back[1]
            imag = imag + map_real * back[1] - map_imag * back[0]
        out_ref[half, 0, :, place] = real
        out_ref[half, 1, :, place] = imag


def consistency_kernel(
    clean_ref,
    maps_ref,
    left_ref,
    columns_twiddle_ref,
    rows_twiddle_ref,
    sampled_ref,
    targets_hbm,
    permute_hbm,
    forward_hbm,
    inverse_hbm,
    right_hbm,
    out_ref,
    raw_ref,
    permute_ref,
    forward_ref,
    inverse_ref,
    right_ref,
    targets_ref,
    clean_halves,
    grad_halves,
    grad_away,
    keep_ref,
    stage_ref,
    sent_first,
    got_first,
    sent_second,
    got_second,
    load_sem,
    send_sem,
    recv_sem,
    pair_sem,
):
    groups, body, _ = stage_ref.shape
    chunks = sent_first.shape[0]
    me = lax.axis_index("gz")
    side = lax.axis_index("col")
    buffers = ((sent_first, got_first), (sent_second, got_second))

    def peer_of(k):
        return lax.rem(me + k, groups)

    def copy(trip, chunk, target, slot):
        sent, got = buffers[trip]
        return pltpu.make_async_remote_copy(
            src_ref=sent.at[chunk, target],
            dst_ref=got.at[chunk, slot],
            send_sem=send_sem.at[trip, chunk, target],
            recv_sem=recv_sem.at[trip, chunk, slot],
            device_id={"gz": target},
            device_id_type=pl.DeviceIdType.MESH,
        )

    def over_peers(action):
        def step(k, carry):
            action(peer_of(k))
            return carry

        lax.fori_loop(1, groups, step, 0)

    def send(trip, chunk):
        sent, got = buffers[trip]
        over_peers(lambda peer: copy(trip, chunk, peer, me).start())
        got[chunk, me] = sent[chunk, me]

    def receive(trip, chunk):
        over_peers(lambda peer: copy(trip, chunk, peer, peer).wait_recv())

    barrier = pltpu.get_barrier_semaphore()
    over_peers(
        lambda peer: pl.semaphore_signal(
            barrier, inc=1, device_id={"gz": peer}, device_id_type=pl.DeviceIdType.MESH
        )
    )
    partner = {"col": 1 - side}
    pl.semaphore_signal(
        barrier, inc=1, device_id=partner, device_id_type=pl.DeviceIdType.MESH
    )
    loads = [
        pltpu.make_async_copy(source, target, load_sem.at[i])
        for i, (source, target) in enumerate(
            (
                (targets_hbm, raw_ref),
                (permute_hbm, permute_ref),
                (forward_hbm, forward_ref),
                (inverse_hbm, inverse_ref),
                (right_hbm, right_ref),
            )
        )
    ]
    for load in loads:
        load.start()
    clean_halves[side] = clean_ref[...]
    pl.semaphore_wait(barrier, groups)
    clean_copy = pltpu.make_async_remote_copy(
        src_ref=clean_ref,
        dst_ref=clean_halves.at[side],
        send_sem=pair_sem.at[0],
        recv_sem=pair_sem.at[1],
        device_id=partner,
        device_id_type=pl.DeviceIdType.MESH,
    )
    clean_copy.start()
    clean_copy.wait()
    for chunk in range(chunks):
        columns_part(chunk, clean_halves, maps_ref, left_ref, columns_twiddle_ref, stage_ref)
        pack(stage_ref, sent_first, chunk)
        send(0, chunk)
    for load in loads:
        load.wait()
    keep_ref[...] = jnp.dot(
        sampled_ref[...], permute_ref[...], preferred_element_type=jnp.float32
    )
    for part in range(2):
        coils = raw_ref.shape[3]
        values = jnp.concatenate(
            [raw_ref[part, :, index, coil, :] for coil in range(coils) for index in range(3)],
            axis=0,
        )
        high = values.astype(jnp.bfloat16)
        low = (values - high.astype(jnp.float32)).astype(jnp.bfloat16)
        targets_ref[part] = jnp.dot(
            high, permute_ref[...], preferred_element_type=jnp.float32
        ) + jnp.dot(low, permute_ref[...], preferred_element_type=jnp.float32)
    for chunk in range(chunks):
        receive(0, chunk)
        rows_part(
            chunk,
            got_first,
            targets_ref,
            keep_ref,
            permute_ref,
            forward_ref,
            inverse_ref,
            rows_twiddle_ref,
            stage_ref,
        )
        pack(stage_ref, sent_second, chunk)
        send(1, chunk)
    for chunk in range(chunks):
        receive(1, chunk)
        combine_part(
            chunk, got_second, maps_ref, right_ref, columns_twiddle_ref, body, grad_halves
        )
    grad_copy = pltpu.make_async_remote_copy(
        src_ref=grad_halves.at[1 - side],
        dst_ref=grad_away,
        send_sem=pair_sem.at[2],
        recv_sem=pair_sem.at[3],
        device_id=partner,
        device_id_type=pl.DeviceIdType.MESH,
    )
    grad_copy.start()
    for trip in range(2):
        for chunk in range(chunks):
            over_peers(lambda peer: copy(trip, chunk, peer, me).wait_send())
    grad_copy.wait()
    out_ref[...] = grad_halves[side] + grad_away[...]


def aligned_gradient(clean, coil_maps, measured, sampled):
    coils, _, rows, full = coil_maps.shape
    groups = lax.axis_size("gz")
    height = rows * groups
    inner = full // 3
    chunks = coils // 2
    body = 2 * 2 * 3 * PIECE
    halves = lax.axis_size("col")
    high, low = pair_matrix(inner, full, False)
    left = np.concatenate([high, high, low], axis=1)
    right = np.concatenate([high, high, low], axis=0)
    rows_high, rows_low = pair_matrix(height // 4, height, True)
    back_high, back_low = pair_matrix(height // 4, height, False)
    forward = np.concatenate([rows_high, rows_high, rows_low], axis=0)
    inverse = np.concatenate([back_high, back_high, back_low], axis=0)
    place = np.arange(height)
    source = place // (height // 4) + 4 * (place % (height // 4))
    permute = (place[:, None] == source[None, :]).astype(jnp.bfloat16)
    targets = measured.reshape(2, PIECE, 3, coils, height)
    keep = jnp.transpose(sampled.reshape(PIECE, 3, height), (1, 0, 2)).astype(jnp.bfloat16)
    keep = keep.reshape(3 * PIECE, height)
    vmem, anywhere = pl.BlockSpec(memory_space=pltpu.VMEM), pl.BlockSpec(memory_space=pl.ANY)
    wire = pltpu.VMEM((chunks, groups, body + 16, rows), jnp.int16)
    return pl.pallas_call(
        consistency_kernel,
        out_shape=jax.ShapeDtypeStruct(clean.shape, jnp.float32),
        in_specs=[vmem] * 6 + [anywhere] * 5,
        out_specs=vmem,
        scratch_shapes=[
            pltpu.VMEM(targets.shape, jnp.float32),
            pltpu.VMEM(permute.shape, jnp.bfloat16),
            pltpu.VMEM(forward.shape, jnp.bfloat16),
            pltpu.VMEM(inverse.shape, jnp.bfloat16),
            pltpu.VMEM(right.shape, jnp.bfloat16),
            pltpu.VMEM((2, coils * 3 * PIECE, height), jnp.float32),
            pltpu.VMEM((halves,) + clean.shape, jnp.float32),
            pltpu.VMEM((halves,) + clean.shape, jnp.float32),
            pltpu.VMEM(clean.shape, jnp.float32),
            pltpu.VMEM(keep.shape, jnp.float32),
            pltpu.VMEM((groups, body, rows), jnp.float32),
            wire,
            wire,
            wire,
            wire,
            pltpu.SemaphoreType.DMA((5,)),
            pltpu.SemaphoreType.DMA((2, chunks, groups)),
            pltpu.SemaphoreType.DMA((2, chunks, groups)),
            pltpu.SemaphoreType.DMA((4,)),
        ],
        compiler_params=pltpu.CompilerParams(
            vmem_limit_bytes=56 * 1024 * 1024, collective_id=0, has_side_effects=True
        ),
        name="consistency",
    )(
        clean,
        coil_maps,
        left,
        twiddle_rows(3, inner),
        twiddle_rows(4, height // 4),
        keep,
        targets,
        permute,
        forward,
        inverse,
        right,
    )


def gradient(clean, coil_maps, measured, sampled):
    coils, _, rows, full = coil_maps.shape
    groups = lax.axis_size("gz")
    whole = rows == 128 and coils % 2 == 0 and full == 3 * PIECE * groups
    whole = whole and lax.axis_size("col") == 2 and full % 768 == 0
    if whole and (rows * groups) % 1024 == 0:
        return aligned_gradient(clean, coil_maps, measured, sampled)
    clean_wide = lax.all_gather(clean, "col", axis=2, tiled=True)
    grad = plain_gradient(clean_wide, coil_maps, measured, sampled)
    return lax.psum_scatter(grad, "col", scatter_dimension=2, tiled=True)


def plain_gradient(clean_wide, coil_maps, measured, sampled):
    maps_real = coil_maps[:, 0]
    maps_imag = coil_maps[:, 1]
    coil_count, row_count, full_cols = maps_real.shape
    coil_pair = complex_mul((maps_real, maps_imag), (clean_wide[0][None], clean_wide[1][None]))
    spectra = transform_last(
        (
            coil_pair[0].reshape(coil_count * row_count, full_cols),
            coil_pair[1].reshape(coil_count * row_count, full_cols),
        ),
        W_FAC,
        -1.0,
    )
    groups = lax.axis_size("gz")
    pencil = full_cols // groups
    arrived = (
        lax.all_to_all(
            spectra[0].reshape(groups, pencil, coil_count, row_count),
            "gz",
            split_axis=0,
            concat_axis=3,
            tiled=True,
        ),
        lax.all_to_all(
            spectra[1].reshape(groups, pencil, coil_count, row_count),
            "gz",
            split_axis=0,
            concat_axis=3,
            tiled=True,
        ),
    )
    item_count = arrived[0].shape[2]
    height = arrived[0].shape[3]
    flattened = (
        arrived[0].reshape(pencil * item_count, height),
        arrived[1].reshape(pencil * item_count, height),
    )
    transformed = transform_last(flattened, H_FAC, -1.0)
    keeping = sampled.astype(jnp.float32)[:, None, :]
    resid_real = keeping * (transformed[0].T.reshape(pencil, item_count, height) - measured[0])
    resid_imag = keeping * (transformed[1].T.reshape(pencil, item_count, height) - measured[1])
    height = resid_real.shape[2]
    inverse = transform_last(
        (
            resid_real.reshape(pencil * coil_count, height),
            resid_imag.reshape(pencil * coil_count, height),
        ),
        H_FAC,
        1.0,
    )
    arrived = (
        lax.all_to_all(
            inverse[0].T.reshape(pencil, coil_count, groups, row_count),
            "gz",
            split_axis=2,
            concat_axis=0,
            tiled=True,
        ),
        lax.all_to_all(
            inverse[1].T.reshape(pencil, coil_count, groups, row_count),
            "gz",
            split_axis=2,
            concat_axis=0,
            tiled=True,
        ),
    )
    item_count = arrived[0].shape[1]
    flattened = (
        arrived[0].reshape(full_cols, item_count * row_count),
        arrived[1].reshape(full_cols, item_count * row_count),
    )
    transformed = transform_first(flattened, W_FAC, 1.0)
    back_real = jnp.transpose(transformed[0].reshape(full_cols, item_count, row_count), (1, 2, 0))
    back_imag = jnp.transpose(transformed[1].reshape(full_cols, item_count, row_count), (1, 2, 0))
    grad_real = jnp.sum(maps_real * back_real + maps_imag * back_imag, axis=0)
    grad_imag = jnp.sum(maps_real * back_imag - maps_imag * back_real, axis=0)
    return jnp.stack([grad_real, grad_imag])


def local(
    noisy_image, fresh_noise, coil_maps, measured, sampled, first_kernel, inner_kernels, last_kernel
):
    predicted = network(noisy_image, first_kernel, inner_kernels, last_kernel)
    clean = (noisy_image - SIGMA_NOW * predicted) / SCALE_NOW
    grad_tile = gradient(clean, coil_maps, measured, sampled)
    update = clean - STEP_GAIN * grad_tile
    return SCALE_NEXT * update + DIRECT_GAIN * predicted + NOISE_GAIN * fresh_noise


def solution(mesh):
    in_specs = (
        P("grp", "gz", "col"),
        P("grp", "gz", "col"),
        P("col", "grp", "gz", None),
        P("grp", "gz", "col", None),
        P("gz", "grp"),
        P(),
        P(),
        P(),
    )
    out_specs = P("grp", "gz", "col")
    return jax.shard_map(local, mesh=mesh, in_specs=in_specs, out_specs=out_specs, check_vma=False)
```
